32 devices in a mesh: wide: 8 (over y, x, core), narrow: 4 (over z).
Axes of the slice: x: 2, y: 2, z: 4, core: 2. Of those that a mesh axis runs over, the one named last changes fastest.
Arguments:
- features: bfloat16 [16384, 512], P(('wide', 'narrow')), may hold values from -6 to 6
- stripe_owner: int32 [4, 2], replicated, may hold values from 0 to 7
- dense_weight: int32 [16384, 1024], P(('wide', 'narrow')), may hold values from 0 to 3
- sparse_weight: int32 [32, 4, 128, 128], P(('wide', 'narrow')), may hold values from 0 to 3
- send_blocks: int32 [32, 4, 2], P(('wide', 'narrow')), may hold values from -1 to 3, as said below
- target_block: int32 [32, 4, 2], P(('wide', 'narrow')), may hold values from 0 to 3
- first_weight: bfloat16 [512, 2048], P('wide'), may hold values from -0.25 to 0.25
- second_weight: bfloat16 [2048, 512], P('wide'), may hold values from -0.125 to 0.125
Outputs:
- updated: bfloat16 [16384, 512], P(('wide', 'narrow'))
The draws below stay inside these ranges and needn't reach their ends.
Inputs may be any that keep to these rules, and one draw needn't show every extreme that they name: `send_blocks`: entry [d, p, s] names a local row block of device d for slot s to partition p of d's wide group, -1 marks an empty slot, filled slots come first; in every wide group one partition receives 2 blocks from every member.
All inputs are finite; a program needn't handle non-finite values.
Results may differ from the reference program's by a relative error of at most 0.0057.
Values may be sent and summed in bfloat16 or wider, within the bound.
No kernel may reach another device: no remote copies, remote signals or barrier semaphores. Data moves between devices by JAX's collectives and lax.ppermute only.
A program may use at most 128 MiB of HBM per device.

```python
import jax
import jax.numpy as jnp
from jax import lax

D = 512
FF = 2048
ROWS = 512
BLOCK = 128
STRIPES = 2
CAP = 2
BLOCKS = 4
DEVICES_ALL = 32
NODES = 16384
N_WIDE = 8
N_NARROW = 4


def draw_send_blocks(key, part):
    key_count = jax.random.fold_in(key, 11)
    key_hot = jax.random.fold_in(key, 12)
    key_pick = jax.random.fold_in(key, 13)
    counts = jax.random.randint(key_count, (DEVICES_ALL, N_NARROW), 0, CAP + 1)
    groups = DEVICES_ALL // N_NARROW
    hottest = jax.random.randint(key_hot, (groups,), 0, N_NARROW)
    group_of = jnp.arange(DEVICES_ALL) // N_NARROW
    column = jnp.arange(N_NARROW)
    is_hot = column[None, :] == hottest[group_of][:, None]
    counts = jnp.where(is_hot, CAP, counts)
    chosen = jax.random.randint(key_pick, (DEVICES_ALL, N_NARROW, CAP), 0, ROWS // BLOCK)
    filled = jnp.arange(CAP)[None, None, :] < counts[:, :, None]
    return jnp.where(filled, chosen, -1).astype(jnp.int32)


def place_ends(drawn, rng, low, top_value):
    dims = drawn.shape
    spot = [jax.random.randint(jax.random.fold_in(rng, axis), (), 0, dims[axis]) for axis in range(len(dims))]
    drawn = drawn.at[tuple(spot)].set(low)
    longest = dims.index(max(dims))
    spot[longest] = (spot[longest] + 1) % dims[longest]
    return drawn.at[tuple(spot)].set(top_value)


def levels(own_key, shape, shards, least, largest):
    def one(axis_at, blocks):
        draws = jax.random.uniform(jax.random.fold_in(jax.random.fold_in(own_key, 6), axis_at), (blocks,), jnp.float32, least / len(shards), largest / len(shards))
        return jnp.repeat(jnp.exp(draws), shape[axis_at] // blocks).reshape((-1,) + (1,) * (len(shape) - axis_at - 1))

    factor_of = one(*shards[0])
    for cut in shards[1:]:
        factor_of = factor_of * one(*cut)
    return factor_of


def normal_values(key, shape, deviation, most, cuts=(), held_as=jnp.bfloat16):
    values = jax.random.normal(key, shape, jnp.float32) * deviation
    if len(cuts) > 0:
        values = levels(key, shape, cuts, -0.22, 0.18) * values
    return jnp.clip(values, min=-most, max=most).astype(held_as)


def setup_inputs(seed: int = 0) -> dict:
    key_of = jax.random.split(jax.random.key(seed), 9)
    return {
        "features": normal_values(key_of[0], (NODES, D), 1.0, 6.0, ((0, 32),)),
        "stripe_owner": place_ends(jax.random.randint(key_of[1], (N_NARROW, STRIPES), 0, N_WIDE), jax.random.fold_in(key_of[1], 1), 0, N_WIDE - 1).astype(jnp.int32),
        "dense_weight": place_ends(jax.random.randint(key_of[2], (NODES, STRIPES * ROWS), 0, 4), jax.random.fold_in(key_of[2], 1), 0, 3).astype(jnp.int32),
        "sparse_weight": place_ends(jax.random.randint(key_of[3], (DEVICES_ALL, N_NARROW, BLOCK, BLOCK), 0, 4), jax.random.fold_in(key_of[3], 1), 0, 3).astype(jnp.int32),
        "send_blocks": draw_send_blocks(jax.random.fold_in(key_of[8], 71), 0),
        "target_block": place_ends(jax.random.randint(key_of[5], (DEVICES_ALL, N_NARROW, CAP), 0, BLOCKS), jax.random.fold_in(key_of[5], 1), 0, BLOCKS - 1).astype(jnp.int32),
        "first_weight": normal_values(key_of[6], (D, FF), D ** -0.5, 0.25, ((0, 8),)),
        "second_weight": normal_values(key_of[7], (FF, D), FF ** -0.5, 0.125, ((0, 8),)),
    }


def reference(features, stripe_owner, dense_weight, sparse_weight, send_blocks, target_block, first_weight, second_weight):
    feature_rows = features.reshape(DEVICES_ALL, ROWS, D)
    block_grid = features.reshape(DEVICES_ALL, BLOCKS, BLOCK, D)
    dense_rows = dense_weight.reshape(DEVICES_ALL, ROWS, STRIPES * ROWS)
    highest = lax.Precision.HIGHEST

    def device_update(device):
        wide_index = device // N_NARROW
        narrow_index = device % N_NARROW
        owners = stripe_owner[narrow_index]
        stripes = feature_rows[owners * N_NARROW + narrow_index].reshape(STRIPES * ROWS, D)
        dense_local = dense_rows[device]
        dense_sum = jnp.dot(dense_local.astype(jnp.bfloat16), stripes, preferred_element_type=jnp.float32)
        source = (wide_index * N_NARROW + jnp.arange(N_NARROW)).astype(jnp.int32)
        listed = send_blocks[source, narrow_index, :]
        present = listed >= 0
        chosen = block_grid[source[:, None], jnp.maximum(listed, 0)]
        tile_weights = sparse_weight[device].astype(jnp.float32)
        products = jnp.einsum('pij,pcjd->pcid', tile_weights, chosen.astype(jnp.float32), precision=highest)
        products = jnp.where(present[:, :, None, None], products, jnp.zeros((), products.dtype))
        routed = (target_block[device][:, :, None] == jnp.arange(BLOCKS)[None, None, :]) & present[:, :, None]
        routed = routed.astype(jnp.float32)
        sparse_sum = jnp.einsum('pcb,pcid->bid', routed, products, precision=highest).reshape(ROWS, D)
        row_weight = lax.optimization_barrier(jnp.sum(tile_weights, axis=2))
        sparse_degree = jnp.einsum('pcb,pi->bi', routed, row_weight, precision=highest).reshape(ROWS)
        degree = 1.0 + lax.optimization_barrier(jnp.sum(dense_local, axis=1)).astype(jnp.float32) + sparse_degree
        combined = (feature_rows[device].astype(jnp.float32) + (dense_sum + sparse_sum) / jnp.sqrt(degree)[:, None]).astype(jnp.bfloat16)
        hidden = jax.nn.relu(jnp.dot(combined, first_weight, preferred_element_type=jnp.float32)).astype(jnp.bfloat16)
        return jnp.dot(hidden, second_weight, preferred_element_type=jnp.float32).astype(jnp.bfloat16)
    updated = lax.map(device_update, jnp.arange(DEVICES_ALL, dtype=jnp.int32))
    return updated.reshape(NODES, D)
```

```python
import functools

import jax
import jax.numpy as jnp
from jax import lax
from jax.experimental import pallas as pl
from jax.experimental.pallas import tpu as pltpu
from jax.sharding import PartitionSpec as P

ABSENT = 64.0
VMEM_LIMIT = 48 * 1024 * 1024


def params():
    return pltpu.CompilerParams(vmem_limit_bytes=VMEM_LIMIT)


def vmem():
    return pl.BlockSpec(memory_space=pltpu.VMEM)


def smem():
    return pl.BlockSpec(memory_space=pltpu.SMEM)


def anywhere():
    return pl.BlockSpec(memory_space=pl.ANY)


def swap(block, count, bit):
    return lax.ppermute(block, "wide", [(i, i ^ bit) for i in range(count)])


def turn(block, count, step):
    return lax.ppermute(block, "narrow", [(i, (i + step) % count) for i in range(count)])


def pick_kernel(parts, cap, block_rows, where_ref, lists_ref, features_ref, *rest):
    outs = rest[: parts - 1]
    empty_ref, sems = rest[parts - 1 :]
    empty_ref[...] = jnp.full(empty_ref.shape, ABSENT, empty_ref.dtype)
    me = where_ref[1]
    copies = []
    for step in range(1, parts):
        to = lax.rem(me + step, parts)
        for slot in range(cap):
            listed = lists_ref[0, to, slot]
            target = outs[step - 1].at[pl.ds(slot * block_rows, block_rows)]
            sem = sems.at[(step - 1) * cap + slot]
            start = pl.multiple_of(jnp.maximum(listed, 0) * block_rows, block_rows)
            real = pltpu.make_async_copy(features_ref.at[pl.ds(start, block_rows)], target, sem)
            blank = pltpu.make_async_copy(empty_ref, target, sem)

            @pl.when(listed >= 0)
            def _():
                real.start()

            @pl.when(listed < 0)
            def _():
                blank.start()

            copies.append(blank)
    for copy in copies:
        copy.wait()


def pick(where, lists, features, block_rows):
    _, parts, cap = lists.shape
    width = features.shape[1]
    shape = jax.ShapeDtypeStruct((cap * block_rows, width), features.dtype)
    return pl.pallas_call(
        functools.partial(pick_kernel, parts, cap, block_rows),
        out_shape=[shape] * (parts - 1),
        in_specs=[smem(), smem(), anywhere()],
        out_specs=[anywhere()] * (parts - 1),
        scratch_shapes=[
            pltpu.VMEM((block_rows, width), features.dtype),
            pltpu.SemaphoreType.DMA(((parts - 1) * cap,)),
        ],
        compiler_params=params(),
        name="pick_blocks",
    )(where, lists, features)


def prepare_kernel(dense_ref, out_ref, degree_ref):
    values = dense_ref[...]
    out_ref[...] = values.astype(jnp.float32).astype(jnp.bfloat16)
    degree_ref[...] = 1.0 + jnp.sum(values, axis=1, keepdims=True).astype(jnp.float32)


def prepare(dense_weight):
    rows, columns = dense_weight.shape
    step = rows // 4
    return pl.pallas_call(
        prepare_kernel,
        grid=(rows // step,),
        out_shape=[
            jax.ShapeDtypeStruct((rows, columns), jnp.bfloat16),
            jax.ShapeDtypeStruct((rows, 1), jnp.float32),
        ],
        in_specs=[pl.BlockSpec((step, columns), lambda i: (i, 0))],
        out_specs=[
            pl.BlockSpec((step, columns), lambda i: (i, 0)),
            pl.BlockSpec((step, 1), lambda i: (i, 0)),
        ],
        compiler_params=params(),
        cost_estimate=pl.CostEstimate(
            flops=2 * rows * columns, bytes_accessed=6 * rows * columns, transcendentals=0
        ),
        name="dense_rows",
    )(dense_weight)


def dense_kernel(where_ref, dense_ref, mine_ref, other_ref, out_ref):
    stripes, half, _ = mine_ref.shape
    core = lax.rem(where_ref[0], 2)
    total = None
    for stripe in range(stripes):
        for ref, side in ((mine_ref, core), (other_ref, 1 - core)):
            start = pl.multiple_of((2 * stripe + side) * half, half)
            part = jnp.dot(
                dense_ref[:, pl.ds(start, half)], ref[stripe], preferred_element_type=jnp.float32
            )
            total = part if total is None else total + part
    out_ref[...] = total


def dense_sum(where, dense, mine, other):
    rows = dense.shape[0]
    stripes, half, width = mine.shape
    return pl.pallas_call(
        dense_kernel,
        out_shape=jax.ShapeDtypeStruct((rows, width), jnp.float32),
        in_specs=[smem(), vmem(), vmem(), vmem()],
        out_specs=vmem(),
        compiler_params=params(),
        cost_estimate=pl.CostEstimate(
            flops=4 * rows * stripes * half * width,
            bytes_accessed=4 * rows * width * 4,
            transcendentals=0,
        ),
        name="dense_product",
    )(where, dense, mine, other)


def load_pieces(me, groups, target_ref, sems):
    copies = []
    for ref, masks in groups:
        rows = ref.shape[1]
        for at, mask in enumerate(masks):
            start = pl.multiple_of((me ^ mask) * rows, rows)
            copy = pltpu.make_async_copy(
                ref.at[at], target_ref.at[pl.ds(start, rows)], sems.at[len(copies)]
            )
            copy.start()
            copies.append(copy)
    return copies


def hidden_kernel(
    parts, cap, masks, where_ref, lists_ref, targets_ref, features_ref, dense_ref, degree_ref,
    tiles_ref, first_a, first_b, *rest
):
    received = rest[: parts - 1]
    out_ref, first_ref, total_ref, count_ref, combined_ref, sems = rest[parts - 1 :]
    me, part = where_ref[0], where_ref[1]
    copies = load_pieces(
        me, ((first_a, masks), (first_b, tuple(mask ^ 1 for mask in masks))), first_ref, sems
    )
    block_rows = tiles_ref.shape[2]
    lanes = count_ref.shape[1]
    total_ref[...] = dense_ref[...]
    count_ref[...] = jnp.broadcast_to(degree_ref[...], count_ref.shape)
    for step in range(parts):
        source = lax.rem(part + parts - step, parts)
        tile = tiles_ref[0, source]
        weight = jnp.sum(tile, axis=1, keepdims=True).astype(jnp.float32)
        tile = tile.astype(jnp.float32).astype(jnp.bfloat16)
        for slot in range(cap):
            if step == 0:
                listed = lists_ref[0, source, slot]
                start = pl.multiple_of(jnp.maximum(listed, 0) * block_rows, block_rows)
                block = features_ref[pl.ds(start, block_rows), :]
                present = jnp.broadcast_to(listed, (1, block.shape[1])) >= 0
            else:
                block = received[step - 1][pl.ds(slot * block_rows, block_rows), :]
                present = block[0:1, :].astype(jnp.float32) < ABSENT / 2
            product = jnp.dot(tile, block, preferred_element_type=jnp.float32)
            product = jnp.where(present, product, 0.0)
            start = pl.multiple_of(targets_ref[0, source, slot] * block_rows, block_rows)
            total_ref[pl.ds(start, block_rows), :] += product
            count_ref[pl.ds(start, block_rows), :] += jnp.where(present[:, :lanes], weight, 0.0)
    scale = lax.rsqrt(count_ref[...])
    for at in range(0, total_ref.shape[1], lanes):
        columns = pl.ds(at, lanes)
        combined_ref[:, columns] = (
            features_ref[:, columns].astype(jnp.float32) + total_ref[:, columns] * scale
        ).astype(jnp.bfloat16)
    for copy in copies:
        copy.wait()
    hidden = out_ref.shape[1]
    step = min(hidden, 512)

    @pl.loop(0, hidden // step)
    def _(at):
        columns = pl.ds(pl.multiple_of(at * step, step), step)
        gated = jnp.dot(
            combined_ref[...], first_ref[:, columns], preferred_element_type=jnp.float32
        )
        out_ref[:, columns] = jnp.maximum(gated, 0.0).astype(jnp.bfloat16)


def hidden_rows(where, lists, targets, features, dense, degree, tiles, first, masks, received):
    rows, width = features.shape
    hidden = first[0].shape[2]
    _, parts, cap = lists.shape
    pieces = 2 * first[0].shape[0]
    return pl.pallas_call(
        functools.partial(hidden_kernel, parts, cap, masks),
        out_shape=jax.ShapeDtypeStruct((rows, hidden), jnp.bfloat16),
        in_specs=[smem(), smem(), smem(), vmem(), vmem(), vmem(), vmem(), anywhere(), anywhere()]
        + [vmem()] * (parts - 1),
        out_specs=vmem(),
        scratch_shapes=[
            pltpu.VMEM((width, hidden), jnp.bfloat16),
            pltpu.VMEM((rows, width), jnp.float32),
            pltpu.VMEM((rows, 128), jnp.float32),
            pltpu.VMEM((rows, width), jnp.bfloat16),
            pltpu.SemaphoreType.DMA((pieces,)),
        ],
        compiler_params=params(),
        cost_estimate=pl.CostEstimate(
            flops=2 * rows * width * hidden, bytes_accessed=8 * rows * hidden, transcendentals=0
        ),
        name="hidden",
    )(where, lists, targets, features, dense, degree, tiles, *first, *received)


def update_kernel(masks, where_ref, hidden_ref, a, b, c, d, out_ref, second_ref, sems):
    me = where_ref[0]
    low, high = masks
    groups = (
        (a, low),
        (b, high),
        (c, tuple(mask ^ 1 for mask in low)),
        (d, tuple(mask ^ 1 for mask in high)),
    )
    for copy in load_pieces(me, groups, second_ref, sems):
        copy.wait()
    width = out_ref.shape[1]
    step = min(width, 256)

    @pl.loop(0, width // step)
    def _(at):
        columns = pl.ds(pl.multiple_of(at * step, step), step)
        out_ref[:, columns] = jnp.dot(
            hidden_ref[...], second_ref[:, columns], preferred_element_type=jnp.float32
        ).astype(jnp.bfloat16)


def update(where, hidden, second, masks):
    rows, depth = hidden.shape
    width = second[0].shape[2]
    pieces = 2 * (len(masks[0]) + len(masks[1]))
    return pl.pallas_call(
        functools.partial(update_kernel, masks),
        out_shape=jax.ShapeDtypeStruct((rows, width), jnp.bfloat16),
        in_specs=[smem(), vmem()] + [anywhere()] * 4,
        out_specs=vmem(),
        scratch_shapes=[
            pltpu.VMEM((depth, width), jnp.bfloat16),
            pltpu.SemaphoreType.DMA((pieces,)),
        ],
        compiler_params=params(),
        cost_estimate=pl.CostEstimate(
            flops=2 * rows * width * depth, bytes_accessed=4 * depth * width, transcendentals=0
        ),
        name="update",
    )(where, hidden, *second)


def shards(
    features,
    stripe_owner,
    dense_weight,
    sparse_weight,
    send_blocks,
    target_block,
    first_weight,
    second_weight,
    wide,
    narrow,
):
    rows = features.shape[0]
    block_rows = sparse_weight.shape[2]
    stripes = stripe_owner.shape[1]
    bits = [1 << at for at in range(1, wide.bit_length() - 1)]
    me, part = lax.axis_index("wide"), lax.axis_index("narrow")
    where = jnp.stack([me, part]).astype(jnp.int32)
    owners = lax.dynamic_index_in_dim(stripe_owner, part, 0, keepdims=False)
    core = me & 1
    half = rows // 2

    first, second = first_weight[None], second_weight[None]
    first_masks, second_masks = (0,), (0,)
    first_new = swap(first, wide, bits[0])
    second_new = swap(second, wide, bits[-1])

    picked = pick(where, send_blocks, features, block_rows)
    received = [turn(block, narrow, step + 1) for step, block in enumerate(picked)]

    kept = lax.dynamic_slice_in_dim(features, core * half, half)
    given = swap(lax.dynamic_slice_in_dim(features, (1 - core) * half, half), wide, 1)
    carried = [jnp.where((owners[k] & 1) == core, kept, given) for k in range(stripes)]
    hops = len(bits)
    for hop in range(hops):
        for k in range(stripes):
            bit = bits[hop] if k % 2 == 0 else bits[hops - 1 - hop]
            came = swap(carried[k], wide, bit)
            carried[k] = jnp.where(((owners[k] ^ me) & bit) == 0, carried[k], came)
    mine = jnp.stack(carried)
    other = swap(mine, wide, 1)

    for hop in range(hops):
        if hop > 0:
            first_new = swap(first, wide, bits[hop])
            second_new = swap(second, wide, bits[hops - 1 - hop])
        first_more = tuple(mask ^ bits[hop] for mask in first_masks)
        second_more = tuple(mask ^ bits[hops - 1 - hop] for mask in second_masks)
        first = jnp.concatenate([first, first_new])
        first_masks += first_more
        if hop < hops - 1:
            second = jnp.concatenate([second, second_new])
            second_masks += second_more
    first_pair = (first, swap(first, wide, 1))
    second_all = (second, second_new, swap(second, wide, 1), swap(second_new, wide, 1))

    dense, degree = prepare(dense_weight)
    dense_total = dense_sum(where, dense, mine, other)
    hidden = hidden_rows(
        where, send_blocks, target_block, features, dense_total, degree, sparse_weight,
        first_pair, first_masks, received,
    )
    return update(where, hidden, second_all, (second_masks, second_more))


def solution(mesh):
    placed = (
        P(("wide", "narrow"), None),
        P(),
        P(("wide", "narrow"), None),
        P(("wide", "narrow"), None, None, None),
        P(("wide", "narrow"), None, None),
        P(("wide", "narrow"), None, None),
        P("wide", None),
        P("wide", None),
    )
    local = functools.partial(shards, wide=mesh.shape["wide"], narrow=mesh.shape["narrow"])
    return jax.shard_map(
        local, mesh=mesh, in_specs=placed, out_specs=P(("wide", "narrow"), None), check_vma=False
    )
```

```python
import functools

import jax
import jax.numpy as jnp
from jax import lax
from jax.experimental import pallas as pl
from jax.experimental.pallas import tpu as pltpu
from jax.sharding import PartitionSpec as P

ABSENT = 64.0
VMEM_LIMIT = 48 * 1024 * 1024


def params():
    return pltpu.CompilerParams(vmem_limit_bytes=VMEM_LIMIT)


def vmem():
    return pl.BlockSpec(memory_space=pltpu.VMEM)


def smem():
    return pl.BlockSpec(memory_space=pltpu.SMEM)


def anywhere():
    return pl.BlockSpec(memory_space=pl.ANY)


def hbm():
    return pl.BlockSpec(memory_space=pltpu.HBM)


def swap(block, count, bit):
    return lax.ppermute(block, "wide", [(i, i ^ bit) for i in range(count)])


def pick_kernel(parts, cap, block_rows, lists_ref, features_ref, out_ref, kept_ref, given_ref, empty_ref, sems):
    empty_ref[...] = jnp.full(empty_ref.shape, ABSENT, empty_ref.dtype)
    core = lax.rem(lax.axis_index("wide"), 2)
    half = kept_ref.shape[0]
    copies = []
    for ref, side in ((given_ref, 1 - core), (kept_ref, core)):
        start = pl.multiple_of(side * half, half)
        copy = pltpu.make_async_copy(
            features_ref.at[pl.ds(start, half)], ref, sems.at[len(copies)]
        )
        copy.start()
        copies.append(copy)
    for to in range(parts):
        for slot in range(cap):
            listed = lists_ref[0, slot, to]
            target = out_ref.at[to, pl.ds(slot * block_rows, block_rows)]
            sem = sems.at[len(copies)]
            start = pl.multiple_of(jnp.maximum(listed, 0) * block_rows, block_rows)
            real = pltpu.make_async_copy(features_ref.at[pl.ds(start, block_rows)], target, sem)
            blank = pltpu.make_async_copy(empty_ref, target, sem)

            @pl.when(listed >= 0)
            def _():
                real.start()

            @pl.when(listed < 0)
            def _():
                blank.start()

            copies.append(blank)
    for copy in copies:
        copy.wait()


def pick(lists, features, block_rows):
    _, cap, parts = lists.shape
    rows, width = features.shape
    half = jax.ShapeDtypeStruct((rows // 2, width), features.dtype)
    return pl.pallas_call(
        functools.partial(pick_kernel, parts, cap, block_rows),
        out_shape=[
            jax.ShapeDtypeStruct((parts, cap * block_rows, width), features.dtype), half, half
        ],
        in_specs=[smem(), hbm()],
        out_specs=[hbm()] * 3,
        scratch_shapes=[
            pltpu.VMEM((block_rows, width), features.dtype),
            pltpu.SemaphoreType.DMA((parts * cap + 2,)),
        ],
        compiler_params=params(),
        name="pick_blocks",
    )(lists, features)


def join_kernel(sizes, *refs):
    sems = refs[-1]
    outs = refs[-1 - len(sizes) : -1]
    copies, at = [], 0
    for stack, size in enumerate(sizes):
        for place in range(size):
            copy = pltpu.make_async_copy(refs[at], outs[stack].at[place], sems.at[at])
            copy.start()
            copies.append(copy)
            at += 1
    for copy in copies:
        copy.wait()


def join(stacks, after):
    flat = [piece for stack in stacks for piece in stack]
    sizes = tuple(len(stack) for stack in stacks)
    return pl.pallas_call(
        functools.partial(join_kernel, sizes),
        out_shape=[
            jax.ShapeDtypeStruct((len(stack),) + stack[0].shape, stack[0].dtype) for stack in stacks
        ],
        in_specs=[hbm()] * len(flat) + [anywhere()] * len(after),
        out_specs=[hbm()] * len(stacks),
        scratch_shapes=[pltpu.SemaphoreType.DMA((len(flat),))],
        compiler_params=params(),
        name="join_pieces",
    )(*flat, *after)


def tie_kernel(*refs):
    pass


def tie(blocks, after):
    return pl.pallas_call(
        tie_kernel,
        out_shape=[jax.ShapeDtypeStruct(block.shape, block.dtype) for block in blocks],
        in_specs=[anywhere()] * (len(blocks) + len(after)),
        out_specs=[anywhere()] * len(blocks),
        input_output_aliases={at: at for at in range(len(blocks))},
        compiler_params=params(),
        name="tie",
    )(*blocks, *after)


def prepare_kernel(dense_ref, out_ref, degree_ref):
    values = dense_ref[...]
    out_ref[...] = values.astype(jnp.float32).astype(jnp.bfloat16)
    degree_ref[...] = 1.0 + jnp.sum(values, axis=1, keepdims=True).astype(jnp.float32)


def prepare(dense_weight):
    rows, columns = dense_weight.shape
    step = rows // 4
    return pl.pallas_call(
        prepare_kernel,
        grid=(rows // step,),
        out_shape=[
            jax.ShapeDtypeStruct((rows, columns), jnp.bfloat16),
            jax.ShapeDtypeStruct((rows, 1), jnp.float32),
        ],
        in_specs=[pl.BlockSpec((step, columns), lambda i: (i, 0))],
        out_specs=[
            pl.BlockSpec((step, columns), lambda i: (i, 0)),
            pl.BlockSpec((step, 1), lambda i: (i, 0)),
        ],
        compiler_params=params(),
        cost_estimate=pl.CostEstimate(
            flops=2 * rows * columns, bytes_accessed=6 * rows * columns, transcendentals=0
        ),
        name="dense_rows",
    )(dense_weight)


def dense_kernel(dense_ref, mine_ref, other_ref, out_ref):
    stripes, half, _ = mine_ref.shape
    core = lax.rem(lax.axis_index("wide"), 2)
    total = None
    for stripe in range(stripes):
        for ref, side in ((mine_ref, core), (other_ref, 1 - core)):
            start = pl.multiple_of((2 * stripe + side) * half, half)
            part = jnp.dot(
                dense_ref[:, pl.ds(start, half)], ref[stripe], preferred_element_type=jnp.float32
            )
            total = part if total is None else total + part
    out_ref[...] = total


def dense_sum(dense, mine, other):
    rows = dense.shape[0]
    stripes, half, width = mine.shape
    return pl.pallas_call(
        dense_kernel,
        out_shape=jax.ShapeDtypeStruct((rows, width), jnp.float32),
        in_specs=[vmem(), vmem(), vmem()],
        out_specs=vmem(),
        compiler_params=params(),
        cost_estimate=pl.CostEstimate(
            flops=4 * rows * stripes * half * width,
            bytes_accessed=4 * rows * width * 4,
            transcendentals=0,
        ),
        name="dense_product",
    )(dense, mine, other)


def load_pieces(refs, masks, target_ref, sems):
    me = lax.axis_index("wide")
    copies = []
    for ref, group in zip(refs, masks):
        for at, mask in enumerate(group):
            source = ref if len(ref.shape) == 2 else ref.at[at]
            rows = source.shape[0]
            start = pl.multiple_of((me ^ mask) * rows, rows)
            copy = pltpu.make_async_copy(
                source, target_ref.at[pl.ds(start, rows)], sems.at[len(copies)]
            )
            copy.start()
            copies.append(copy)
    return copies


def combine_kernel(
    parts, cap, targets_ref, features_ref, dense_ref, degree_ref, tiles_ref, received_ref, out_ref,
    total_ref, count_ref
):
    block_rows = tiles_ref.shape[2]
    lanes = count_ref.shape[1]
    total_ref[...] = dense_ref[...]
    count_ref[...] = jnp.broadcast_to(degree_ref[...], count_ref.shape)
    for source in range(parts):
        tile = tiles_ref[0, source]
        weight = jnp.sum(tile, axis=1, keepdims=True).astype(jnp.float32)
        tile = tile.astype(jnp.float32).astype(jnp.bfloat16)
        for slot in range(cap):
            block = received_ref[source, pl.ds(slot * block_rows, block_rows), :]
            present = block[0:1, :].astype(jnp.float32) < ABSENT / 2
            product = jnp.dot(tile, block, preferred_element_type=jnp.float32)
            product = jnp.where(present, product, 0.0)
            start = pl.multiple_of(targets_ref[0, slot, source] * block_rows, block_rows)
            total_ref[pl.ds(start, block_rows), :] += product
            count_ref[pl.ds(start, block_rows), :] += jnp.where(present[:, :lanes], weight, 0.0)
    scale = lax.rsqrt(count_ref[...])
    for at in range(0, total_ref.shape[1], lanes):
        columns = pl.ds(at, lanes)
        out_ref[:, columns] = (
            features_ref[:, columns].astype(jnp.float32) + total_ref[:, columns] * scale
        ).astype(jnp.bfloat16)


def combine(targets, features, dense, degree, tiles, received):
    rows, width = features.shape
    _, cap, parts = targets.shape
    return pl.pallas_call(
        functools.partial(combine_kernel, parts, cap),
        out_shape=jax.ShapeDtypeStruct((rows, width), jnp.bfloat16),
        in_specs=[smem()] + [vmem()] * 5,
        out_specs=vmem(),
        scratch_shapes=[
            pltpu.VMEM((rows, width), jnp.float32),
            pltpu.VMEM((rows, 128), jnp.float32),
        ],
        compiler_params=params(),
        cost_estimate=pl.CostEstimate(
            flops=4 * rows * width * tiles.shape[2], bytes_accessed=8 * rows * width,
            transcendentals=0,
        ),
        name="combine",
    )(targets, features, dense, degree, tiles, received)


def perceptron_kernel(first_masks, second_masks, combined_ref, *refs):
    out_ref, first_ref, second_ref, hidden_ref, first_sems, second_sems = refs[-6:]
    count = len(first_masks)
    first_copies = load_pieces(refs[:count], first_masks, first_ref, first_sems)
    second_copies = load_pieces(refs[count:-6], second_masks, second_ref, second_sems)
    for copy in first_copies:
        copy.wait()
    hidden = hidden_ref.shape[1]
    step = min(hidden, 512)

    @pl.loop(0, hidden // step)
    def _(at):
        columns = pl.ds(pl.multiple_of(at * step, step), step)
        gated = jnp.dot(
            combined_ref[...], first_ref[:, columns], preferred_element_type=jnp.float32
        )
        hidden_ref[:, columns] = jnp.maximum(gated, 0.0).astype(jnp.bfloat16)

    for copy in second_copies:
        copy.wait()
    width = out_ref.shape[1]
    wide_step = min(width, 256)

    @pl.loop(0, width // wide_step)
    def _(at):
        columns = pl.ds(pl.multiple_of(at * wide_step, wide_step), wide_step)
        out_ref[:, columns] = jnp.dot(
            hidden_ref[...], second_ref[:, columns], preferred_element_type=jnp.float32
        ).astype(jnp.bfloat16)


def perceptron(combined, first, first_masks, second, second_masks):
    rows, width = combined.shape
    hidden = first[0].shape[-1]
    return pl.pallas_call(
        functools.partial(perceptron_kernel, first_masks, second_masks),
        out_shape=jax.ShapeDtypeStruct((rows, width), jnp.bfloat16),
        in_specs=[vmem()] + [hbm()] * (len(first) + len(second)),
        out_specs=vmem(),
        scratch_shapes=[
            pltpu.VMEM((width, hidden), jnp.bfloat16),
            pltpu.VMEM((hidden, width), jnp.bfloat16),
            pltpu.VMEM((rows, hidden), jnp.bfloat16),
            pltpu.SemaphoreType.DMA((sum(len(group) for group in first_masks),)),
            pltpu.SemaphoreType.DMA((sum(len(group) for group in second_masks),)),
        ],
        compiler_params=params(),
        cost_estimate=pl.CostEstimate(
            flops=4 * rows * width * hidden, bytes_accessed=4 * width * hidden, transcendentals=0
        ),
        name="perceptron",
    )(combined, *first, *second)


def first_pieces(shard, wide, order):
    pieces = {0: shard}
    for bit in order:
        pieces[bit] = swap(shard, wide, bit)
    return pieces


def other_pieces(pieces, wide, order):
    late = {}
    known = [order[0]]
    for bit in order[1:]:
        for mask in known:
            held = late[mask] if mask in late else pieces[mask]
            late[mask ^ bit] = swap(held, wide, bit)
        known = known + [bit] + [mask ^ bit for mask in known]
    return late


def crossed(masks):
    return tuple(mask ^ 1 for mask in masks)


def shards(
    features,
    stripe_owner,
    dense_weight,
    sparse_weight,
    send_blocks,
    target_block,
    first_weight,
    second_weight,
    wide,
    narrow,
):
    block_rows = sparse_weight.shape[2]
    stripes = stripe_owner.shape[1]
    bits = [1 << at for at in range(1, wide.bit_length() - 1)]
    orders = (bits, bits[::-1])
    hops = len(bits)
    me, part = lax.axis_index("wide"), lax.axis_index("narrow")
    owners = lax.dynamic_index_in_dim(stripe_owner, part, 0, keepdims=False)
    core = me & 1
    lists = jnp.transpose(send_blocks, (0, 2, 1))
    targets = jnp.transpose(target_block, (0, 2, 1))

    weights = [
        first_pieces(shard, wide, order)
        for shard, order in zip((first_weight, second_weight), orders)
    ]
    picked, kept, given = pick(lists, features, block_rows)
    received = lax.all_to_all(picked, "narrow", 0, 0)

    given = swap(given, wide, 1)
    carried = [jnp.where((owners[k] & 1) == core, kept, given) for k in range(stripes)]
    for hop in range(hops):
        for k in range(stripes):
            bit = orders[k % 2][hop]
            came = swap(carried[k], wide, bit)
            carried[k] = jnp.where(((owners[k] ^ me) & bit) == 0, carried[k], came)
    mine = jnp.stack(carried)
    other = swap(mine, wide, 1)

    dense, degree = prepare(dense_weight)

    early_masks = [tuple(pieces) for pieces in weights]
    stacks = join([list(pieces.values()) for pieces in weights], [degree])
    crossed_stacks = [swap(stack, wide, 1) for stack in stacks]
    forward = tie(
        [pieces[mask] for pieces, order in zip(weights, orders) for mask in order[:-1]],
        crossed_stacks,
    )
    at = 0
    for pieces, order in zip(weights, orders):
        for mask in order[:-1]:
            pieces[mask] = forward[at]
            at += 1
    more = [other_pieces(pieces, wide, order) for pieces, order in zip(weights, orders)]
    ends = [
        list(pieces.values())[0] if len(pieces) == 1 else jnp.stack(list(pieces.values()))
        for pieces in more
    ]
    more_masks = [tuple(pieces) for pieces in more]
    refs, masks = [], []
    for at in range(2):
        refs.append((stacks[at], crossed_stacks[at], ends[at], swap(ends[at], wide, 1)))
        masks.append(
            (early_masks[at], crossed(early_masks[at]), more_masks[at], crossed(more_masks[at]))
        )

    dense_total = dense_sum(dense, mine, other)
    combined = combine(targets, features, dense_total, degree, sparse_weight, received)
    return perceptron(combined, refs[0], masks[0], refs[1], masks[1])


def solution(mesh):
    placed = (
        P(("wide", "narrow"), None),
        P(),
        P(("wide", "narrow"), None),
        P(("wide", "narrow"), None, None, None),
        P(("wide", "narrow"), None, None),
        P(("wide", "narrow"), None, None),
        P("wide", None),
        P("wide", None),
    )
    local = functools.partial(shards, wide=mesh.shape["wide"], narrow=mesh.shape["narrow"])
    return jax.shard_map(
        local, mesh=mesh, in_specs=placed, out_specs=P(("wide", "narrow"), None), check_vma=False
    )
```

```python
import functools

import jax
import jax.numpy as jnp
from jax import lax
from jax.experimental import pallas as pl
from jax.experimental.pallas import tpu as pltpu
from jax.sharding import PartitionSpec as P

LANES = 128
ABSENT = 64.0
VMEM_LIMIT = 48 * 1024 * 1024
SLACK = 0
LARGE_LIMIT = 48 * 1024 * 1024
SLACK_BLOCKS = 0
LAYER_LIMIT = 52 * 1024 * 1024
SLACK_STRIPES = 4 * 10**9


def params(limit=VMEM_LIMIT):
    return pltpu.CompilerParams(vmem_limit_bytes=limit)


def vmem():
    return pl.BlockSpec(memory_space=pltpu.VMEM)


def smem():
    return pl.BlockSpec(memory_space=pltpu.SMEM)


def anywhere():
    return pl.BlockSpec(memory_space=pl.ANY)


def hbm():
    return pl.BlockSpec(memory_space=pltpu.HBM)


def swap(block, count, bit):
    return lax.ppermute(block, "wide", [(i, i ^ bit) for i in range(count)])


def pick_kernel(parts, cap, block_rows, lists_ref, features_ref, out_ref, empty_ref, sems):
    empty_ref[...] = jnp.full(empty_ref.shape, ABSENT, empty_ref.dtype)
    copies = []
    for to in range(parts):
        for slot in range(cap):
            listed = lists_ref[0, slot, to]
            target = out_ref.at[to, pl.ds(slot * block_rows, block_rows)]
            sem = sems.at[len(copies)]
            start = pl.multiple_of(jnp.maximum(listed, 0) * block_rows, block_rows)
            real = pltpu.make_async_copy(features_ref.at[pl.ds(start, block_rows)], target, sem)
            blank = pltpu.make_async_copy(empty_ref, target, sem)

            @pl.when(listed >= 0)
            def _():
                real.start()

            @pl.when(listed < 0)
            def _():
                blank.start()

            copies.append(blank)
    for copy in copies:
        copy.wait()


def pick(lists, features, block_rows):
    _, cap, parts = lists.shape
    width = features.shape[1]
    return pl.pallas_call(
        functools.partial(pick_kernel, parts, cap, block_rows),
        out_shape=jax.ShapeDtypeStruct((parts, cap * block_rows, width), features.dtype),
        in_specs=[smem(), hbm()],
        out_specs=hbm(),
        scratch_shapes=[
            pltpu.VMEM((block_rows, width), features.dtype),
            pltpu.SemaphoreType.DMA((parts * cap,)),
        ],
        compiler_params=params(LARGE_LIMIT),
        name="pick_blocks",
    )(lists, features)


def halves_kernel(owners_ref, mine_ref, other_ref, *rest):
    outs, sems = rest[:-1], rest[-1]
    core, part = lax.rem(lax.axis_index("wide"), 2), lax.axis_index("narrow")
    half = outs[0].shape[0]
    rows = pl.ds(pl.multiple_of(core * half, half), half)
    copies = []
    for k, out in enumerate(outs):
        own = (owners_ref[k, part] & 1) == core
        kept = pltpu.make_async_copy(mine_ref.at[rows], out, sems.at[k])
        came = pltpu.make_async_copy(other_ref.at[rows], out, sems.at[k])

        @pl.when(own)
        def _():
            kept.start()

        @pl.when(jnp.logical_not(own))
        def _():
            came.start()

        copies.append(kept)
    for copy in copies:
        copy.wait()


def halves(owners, mine, other):
    rows, width = mine.shape
    stripes = owners.shape[0]
    return pl.pallas_call(
        halves_kernel,
        out_shape=[jax.ShapeDtypeStruct((rows // 2, width), mine.dtype)] * stripes,
        in_specs=[smem(), anywhere(), anywhere()],
        out_specs=[anywhere()] * stripes,
        scratch_shapes=[pltpu.SemaphoreType.DMA((stripes,))],
        compiler_params=params(),
        name="stripe_halves",
    )(owners, mine, other)


def choose_kernel(bits, stacked, others, owners_ref, *refs):
    count = len(bits)
    refs = refs[: 2 * count] + refs[2 * count + others :]
    sems = refs[-1]
    me, part = lax.axis_index("wide"), lax.axis_index("narrow")
    copies = []
    for k, bit in enumerate(bits):
        out = refs[2 * count].at[k] if stacked else refs[2 * count + k]
        same = ((owners_ref[k, part] ^ me) & bit) == 0
        kept = pltpu.make_async_copy(refs[k], out, sems.at[k])
        came = pltpu.make_async_copy(refs[count + k], out, sems.at[k])

        @pl.when(same)
        def _():
            kept.start()

        @pl.when(jnp.logical_not(same))
        def _():
            came.start()

        copies.append(kept)
    for copy in copies:
        copy.wait()


def choose(owners, bits, carried, came, stacked, after):
    count = len(bits)
    shape, dtype = carried[0].shape, carried[0].dtype
    if stacked:
        out_shape, out_specs = jax.ShapeDtypeStruct((count,) + shape, dtype), anywhere()
    else:
        out_shape, out_specs = [jax.ShapeDtypeStruct(shape, dtype)] * count, [anywhere()] * count
    return pl.pallas_call(
        functools.partial(choose_kernel, bits, stacked, len(after)),
        out_shape=out_shape,
        in_specs=[smem()] + [anywhere()] * (2 * count + len(after)),
        out_specs=out_specs,
        scratch_shapes=[pltpu.SemaphoreType.DMA((count,))],
        compiler_params=params(),
        name="stripe_choice",
    )(owners, *carried, *came, *after)


def pack_kernel(first_ref, second_ref, out_ref, sems):
    rows, width = first_ref.shape[0], out_ref.shape[2]
    copies = [pltpu.make_async_copy(second_ref, out_ref.at[1], sems.at[0])]
    for at in range(first_ref.shape[1] // width):
        copies.append(
            pltpu.make_async_copy(
                first_ref.at[:, pl.ds(at * width, width)],
                out_ref.at[0, pl.ds(at * rows, rows)],
                sems.at[1 + at],
            )
        )
    for copy in copies:
        copy.start()
    for copy in copies:
        copy.wait()


def pack(first, second):
    blocks = first.shape[1] // second.shape[1]
    return pl.pallas_call(
        pack_kernel,
        out_shape=jax.ShapeDtypeStruct((2,) + second.shape, second.dtype),
        in_specs=[hbm()] * 2,
        out_specs=hbm(),
        scratch_shapes=[pltpu.SemaphoreType.DMA((1 + blocks,))],
        compiler_params=params(LARGE_LIMIT),
        name="pack_weights",
    )(first, second)


def split_kernel(parts, count, *refs):
    ins, stack_ref, outs, sems = refs[:count], refs[-2 - len(parts)], refs[-1 - len(parts) : -1], refs[-1]
    copies = []
    for out, (at, part) in zip(outs, parts):
        copies.append(pltpu.make_async_copy(ins[at].at[part], out, sems.at[len(copies)]))
    for at in range(count):
        copies.append(pltpu.make_async_copy(ins[at], stack_ref.at[at], sems.at[len(copies)]))
    for copy in copies:
        copy.start()
    for copy in copies:
        copy.wait()


def split(packs, parts, after):
    shape, dtype = packs[0].shape, packs[0].dtype
    stack, *outs = pl.pallas_call(
        functools.partial(split_kernel, parts, len(packs)),
        out_shape=[jax.ShapeDtypeStruct((len(packs),) + shape, dtype)]
        + [jax.ShapeDtypeStruct(shape[1:], dtype)] * len(parts),
        in_specs=[anywhere()] * (len(packs) + len(after)),
        out_specs=[anywhere()] * (1 + len(parts)),
        scratch_shapes=[pltpu.SemaphoreType.DMA((len(parts) + len(packs),))],
        compiler_params=params(),
        name="split_packs",
    )(*packs, *after)
    return stack, outs


def tie_kernel(*refs):
    pass


def tie(blocks, after, work=0):
    return pl.pallas_call(
        tie_kernel,
        out_shape=[jax.ShapeDtypeStruct(block.shape, block.dtype) for block in blocks],
        in_specs=[anywhere()] * (len(blocks) + len(after)),
        out_specs=[anywhere()] * len(blocks),
        input_output_aliases={at: at for at in range(len(blocks))},
        compiler_params=params(),
        cost_estimate=pl.CostEstimate(flops=work, bytes_accessed=0, transcendentals=0),
        name="tie",
    )(*blocks, *after)


def prepare_kernel(dense_ref, out_ref, degree_ref):
    values = dense_ref[...]
    out_ref[...] = values.astype(jnp.float32).astype(jnp.bfloat16)
    sums = 1.0 + jnp.sum(values, axis=1, keepdims=True).astype(jnp.float32)
    degree_ref[...] = jnp.broadcast_to(sums, degree_ref.shape)


def prepare(dense_weight):
    rows, columns = dense_weight.shape
    step = rows // 4
    return pl.pallas_call(
        prepare_kernel,
        grid=(rows // step,),
        out_shape=[
            jax.ShapeDtypeStruct((rows, columns), jnp.bfloat16),
            jax.ShapeDtypeStruct((rows, LANES), jnp.float32),
        ],
        in_specs=[pl.BlockSpec((step, columns), lambda i: (i, 0))],
        out_specs=[
            pl.BlockSpec((step, columns), lambda i: (i, 0)),
            pl.BlockSpec((step, LANES), lambda i: (i, 0)),
        ],
        compiler_params=params(),
        cost_estimate=pl.CostEstimate(
            flops=2 * rows * columns, bytes_accessed=6 * rows * columns, transcendentals=0
        ),
        name="dense_rows",
    )(dense_weight)


def add_stripes(dense_ref, mine_ref, other_ref, total_ref):
    stripes, half, _ = mine_ref.shape
    core = lax.rem(lax.axis_index("wide"), 2)
    total = None
    for stripe in range(stripes):
        for ref, side in ((mine_ref, core), (other_ref, 1 - core)):
            start = pl.multiple_of((2 * stripe + side) * half, half)
            part = jnp.dot(
                dense_ref[:, pl.ds(start, half)], ref[stripe], preferred_element_type=jnp.float32
            )
            total = part if total is None else total + part
    total_ref[...] = total


def add_blocks(targets_ref, tiles_ref, received_ref, total_ref, count_ref):
    _, parts, block_rows, _ = tiles_ref.shape
    for source in range(parts):
        tile = tiles_ref[0, source]
        weight = jnp.sum(tile, axis=1, keepdims=True).astype(jnp.float32)
        tile = tile.astype(jnp.float32).astype(jnp.bfloat16)
        for slot in range(received_ref.shape[1] // block_rows):
            block = received_ref[source, pl.ds(slot * block_rows, block_rows), :]
            present = block[0:1, :].astype(jnp.float32) < ABSENT / 2
            product = jnp.dot(tile, block, preferred_element_type=jnp.float32)
            product = jnp.where(present, product, 0.0)
            start = pl.multiple_of(targets_ref[0, slot, source] * block_rows, block_rows)
            total_ref[pl.ds(start, block_rows), :] += product
            count_ref[pl.ds(start, block_rows), :] += jnp.where(present[:, :LANES], weight, 0.0)


def combine(features_ref, total_ref, count_ref, combined_ref):
    scale = lax.rsqrt(count_ref[...])
    for at in range(0, total_ref.shape[1], LANES):
        columns = pl.ds(at, LANES)
        combined_ref[:, columns] = (
            features_ref[:, columns].astype(jnp.float32) + total_ref[:, columns] * scale
        ).astype(jnp.bfloat16)


def place_first(pieces, first_ref):
    me, blocks = lax.axis_index("wide"), first_ref.shape[0]
    for ref, mask in pieces:
        rows = ref.shape[0] // blocks
        start = pl.multiple_of((me ^ mask) * rows, rows)
        for at in range(blocks):
            first_ref[at, pl.ds(start, rows), :] = ref[pl.ds(at * rows, rows), :]


def place_second(pieces, second_ref):
    me = lax.axis_index("wide")
    for ref, mask in pieces:
        rows = ref.shape[0]
        second_ref[pl.ds(pl.multiple_of((me ^ mask) * rows, rows), rows), :] = ref[...]


def layer_kernel(own, came, late, targets_ref, *refs):
    count = 7 + len(own) + len(came) + len(late)
    held = refs[count + 1 : 2 * count + 1]
    out_ref = refs[count]
    first_ref, second_ref, hidden_ref, total_ref, combined_ref, sems = refs[2 * count + 1 :]
    copies = [
        pltpu.make_async_copy(ref, target, sems.at[at])
        for at, (ref, target) in enumerate(zip(refs[:count], held))
    ]
    for copy in copies:
        copy.start()
    dense_ref, mine_ref, other_ref, count_ref, tiles_ref, received_ref, features_ref = held[:7]
    packs = list(zip(held[7:], own))
    for ref, masks in zip(held[7 + len(own) :], came):
        packs += [(ref.at[at], mask) for at, mask in enumerate(masks)]
    pieces = [[(ref.at[which], mask) for ref, mask in packs] for which in range(2)]
    for ref, (which, masks) in zip(held[7 + len(own) + len(came) :], late):
        pieces[which] += [
            (ref if len(masks) == 1 else ref.at[at], mask) for at, mask in enumerate(masks)
        ]
    for copy in copies[:3]:
        copy.wait()
    add_stripes(dense_ref, mine_ref, other_ref, total_ref)
    for copy in copies[3:7]:
        copy.wait()
    add_blocks(targets_ref, tiles_ref, received_ref, total_ref, count_ref)
    combine(features_ref, total_ref, count_ref, combined_ref)
    for copy in copies[7:]:
        copy.wait()
    place_first(pieces[0], first_ref)
    width = first_ref.shape[2]
    for at in range(first_ref.shape[0]):
        gated = jnp.dot(combined_ref[...], first_ref[at], preferred_element_type=jnp.float32)
        hidden_ref[:, pl.ds(at * width, width)] = jnp.maximum(gated, 0.0).astype(jnp.bfloat16)
    place_second(pieces[1], second_ref)
    out_ref[...] = jnp.dot(
        hidden_ref[...], second_ref[...], preferred_element_type=jnp.float32
    ).astype(jnp.bfloat16)


def layer(targets, arrays, own, came, late, count):
    features = arrays[-1]
    rows, width = features.shape
    refs = list(arrays) + [block for block, _ in own + came] + [block for block, _, _ in late]
    depth = own[0][0].shape[1] * count
    return pl.pallas_call(
        functools.partial(
            layer_kernel,
            tuple(mask for _, mask in own),
            tuple(masks for _, masks in came),
            tuple((which, masks) for _, which, masks in late),
        ),
        out_shape=jax.ShapeDtypeStruct((rows, width), jnp.bfloat16),
        in_specs=[smem()] + [anywhere()] * len(refs),
        out_specs=vmem(),
        scratch_shapes=[pltpu.VMEM(ref.shape, ref.dtype) for ref in refs]
        + [
            pltpu.VMEM((depth // width, width, width), jnp.bfloat16),
            pltpu.VMEM((depth, width), jnp.bfloat16),
            pltpu.VMEM((rows, depth), jnp.bfloat16),
            pltpu.VMEM((rows, width), jnp.float32),
            pltpu.VMEM((rows, width), jnp.bfloat16),
            pltpu.SemaphoreType.DMA((len(refs),)),
        ],
        compiler_params=params(LAYER_LIMIT),
        cost_estimate=pl.CostEstimate(
            flops=4 * rows * width * depth, bytes_accessed=4 * width * depth, transcendentals=0
        ),
        name="layer",
    )(targets, *refs)


def other_pieces(pieces, wide, order):
    late = {}
    known = [order[0]]
    for bit in order[1:]:
        for mask in known:
            held = late[mask] if mask in late else pieces[mask]
            late[mask ^ bit] = swap(held, wide, bit)
        known = known + [bit] + [mask ^ bit for mask in known]
    return late


def crossed(masks):
    return tuple(mask ^ 1 for mask in masks)


def shards(
    features,
    stripe_owner,
    dense_weight,
    sparse_weight,
    send_blocks,
    target_block,
    first_weight,
    second_weight,
    wide,
    narrow,
):
    block_rows = sparse_weight.shape[2]
    stripes = stripe_owner.shape[1]
    bits = [1 << at for at in range(1, wide.bit_length() - 1)]
    orders = (bits, bits[::-1])
    hops = len(bits)
    owners = jnp.transpose(stripe_owner)
    lists = jnp.transpose(send_blocks, (0, 2, 1))
    targets = jnp.transpose(target_block, (0, 2, 1))

    own = pack(first_weight, second_weight)
    packs = [swap(own, wide, bit) for bit in bits]
    received = lax.all_to_all(pick(lists, features, block_rows), "narrow", 0, 0)
    (received,) = tie([received], [], SLACK_BLOCKS)

    dense, degree = prepare(dense_weight)

    carried = halves(owners, features, swap(features, wide, 1))
    along = [tuple(orders[k % 2][hop] for k in range(stripes)) for hop in range(hops)]
    came = [swap(block, wide, bit) for block, bit in zip(carried, along[0])]

    own_crossed = swap(own, wide, 1)
    parts = [(bits.index(bit), which) for which in range(2) for bit in orders[which][:-1]]
    stack, forward = split(packs, tuple(parts), [own_crossed] + list(carried))
    masks = tuple(bits)
    stacks = [(stack, masks), (swap(stack, wide, 1), crossed(masks))]
    ends, end_masks = [], []
    for which in range(2):
        held = {bits[at]: block for (at, of), block in zip(parts, forward) if of == which}
        late = other_pieces(held, wide, orders[which])
        blocks = list(late.values())
        ends.append(blocks[0] if len(blocks) == 1 else jnp.stack(blocks))
        end_masks.append(tuple(late))

    for hop in range(1, hops):
        carried = choose(owners, along[hop - 1], carried, came, False, [degree, stack])
        came = [swap(block, wide, bit) for block, bit in zip(carried, along[hop])]
    carried = choose(owners, along[-1], carried, came, True, ends)
    (other,) = tie([swap(carried, wide, 1)], [], SLACK_STRIPES)

    ends = tie(ends, [stacks[1][0]])
    crossed_ends = tie([swap(end, wide, 1) for end in ends], [], SLACK)
    late = []
    for which in range(2):
        late.append((ends[which], which, end_masks[which]))
        late.append((crossed_ends[which], which, crossed(end_masks[which])))

    arrays = (dense, carried, other, degree, sparse_weight, received, features)
    return layer(targets, arrays, [(own, 0), (own_crossed, 1)], stacks, late, wide)


def solution(mesh):
    placed = (
        P(("wide", "narrow"), None),
        P(),
        P(("wide", "narrow"), None),
        P(("wide", "narrow"), None, None, None),
        P(("wide", "narrow"), None, None),
        P(("wide", "narrow"), None, None),
        P("wide", None),
        P("wide", None),
    )
    local = functools.partial(shards, wide=mesh.shape["wide"], narrow=mesh.shape["narrow"])
    return jax.shard_map(
        local, mesh=mesh, in_specs=placed, out_specs=P(("wide", "narrow"), None), check_vma=False
    )
```

```python
import functools

import jax
import jax.numpy as jnp
from jax import lax
from jax.experimental import pallas as pl
from jax.experimental.pallas import tpu as pltpu
from jax.sharding import PartitionSpec as P

LANES = 128
ABSENT = 64.0
VMEM_LIMIT = 48 * 1024 * 1024
LARGE_LIMIT = 48 * 1024 * 1024
SLACK_WEIGHTS = 0
ROWS_FLOPS = 10**9
ROWS_LIMIT = 48 * 2**20
LAYER_FLOPS = 10**11
LAYER_BYTES = 4 * 10**6
LAYER_LIMIT = 48 * 2**20
SLACK_STRIPES = 2 * 10**9


def params(limit=VMEM_LIMIT):
    return pltpu.CompilerParams(vmem_limit_bytes=limit)


def vmem():
    return pl.BlockSpec(memory_space=pltpu.VMEM)


def smem():
    return pl.BlockSpec(memory_space=pltpu.SMEM)


def anywhere():
    return pl.BlockSpec(memory_space=pl.ANY)


def hbm():
    return pl.BlockSpec(memory_space=pltpu.HBM)


def swap(block, count, bit):
    return lax.ppermute(block, "wide", [(i, i ^ bit) for i in range(count)])


def pick_kernel(parts, cap, block_rows, lists_ref, features_ref, out_ref, empty_ref, sems):
    empty_ref[...] = jnp.full(empty_ref.shape, ABSENT, empty_ref.dtype)
    copies = []
    for to in range(parts):
        for slot in range(cap):
            listed = lists_ref[0, slot, to]
            target = out_ref.at[to, pl.ds(slot * block_rows, block_rows)]
            sem = sems.at[len(copies)]
            start = pl.multiple_of(jnp.maximum(listed, 0) * block_rows, block_rows)
            real = pltpu.make_async_copy(features_ref.at[pl.ds(start, block_rows)], target, sem)
            blank = pltpu.make_async_copy(empty_ref, target, sem)

            @pl.when(listed >= 0)
            def _():
                real.start()

            @pl.when(listed < 0)
            def _():
                blank.start()

            copies.append(blank)
    for copy in copies:
        copy.wait()


def pick(lists, features, block_rows):
    _, cap, parts = lists.shape
    width = features.shape[1]
    return pl.pallas_call(
        functools.partial(pick_kernel, parts, cap, block_rows),
        out_shape=jax.ShapeDtypeStruct((parts, cap * block_rows, width), features.dtype),
        in_specs=[smem(), hbm()],
        out_specs=hbm(),
        scratch_shapes=[
            pltpu.VMEM((block_rows, width), features.dtype),
            pltpu.SemaphoreType.DMA((parts * cap,)),
        ],
        compiler_params=params(LARGE_LIMIT),
        name="pick_blocks",
    )(lists, features)


def halves_kernel(owners_ref, mine_ref, other_ref, *rest):
    outs, sems = rest[:-1], rest[-1]
    core, part = lax.rem(lax.axis_index("wide"), 2), lax.axis_index("narrow")
    half = outs[0].shape[0]
    rows = pl.ds(pl.multiple_of(core * half, half), half)
    copies = []
    for k, out in enumerate(outs):
        own = (owners_ref[k, part] & 1) == core
        kept = pltpu.make_async_copy(mine_ref.at[rows], out, sems.at[k])
        came = pltpu.make_async_copy(other_ref.at[rows], out, sems.at[k])

        @pl.when(own)
        def _():
            kept.start()

        @pl.when(jnp.logical_not(own))
        def _():
            came.start()

        copies.append(kept)
    for copy in copies:
        copy.wait()


def halves(owners, mine, other):
    rows, width = mine.shape
    stripes = owners.shape[0]
    return pl.pallas_call(
        halves_kernel,
        out_shape=[jax.ShapeDtypeStruct((rows // 2, width), mine.dtype)] * stripes,
        in_specs=[smem(), anywhere(), anywhere()],
        out_specs=[anywhere()] * stripes,
        scratch_shapes=[pltpu.SemaphoreType.DMA((stripes,))],
        compiler_params=params(),
        name="stripe_halves",
    )(owners, mine, other)


def choose_kernel(bits, stacked, others, owners_ref, *refs):
    count = len(bits)
    refs = refs[: 2 * count] + refs[2 * count + others :]
    sems = refs[-1]
    me, part = lax.axis_index("wide"), lax.axis_index("narrow")
    copies = []
    for k, bit in enumerate(bits):
        out = refs[2 * count].at[k] if stacked else refs[2 * count + k]
        same = ((owners_ref[k, part] ^ me) & bit) == 0
        kept = pltpu.make_async_copy(refs[k], out, sems.at[k])
        came = pltpu.make_async_copy(refs[count + k], out, sems.at[k])

        @pl.when(same)
        def _():
            kept.start()

        @pl.when(jnp.logical_not(same))
        def _():
            came.start()

        copies.append(kept)
    for copy in copies:
        copy.wait()


def choose(owners, bits, carried, came, stacked, after):
    count = len(bits)
    shape, dtype = carried[0].shape, carried[0].dtype
    if stacked:
        out_shape, out_specs = jax.ShapeDtypeStruct((count,) + shape, dtype), anywhere()
    else:
        out_shape, out_specs = [jax.ShapeDtypeStruct(shape, dtype)] * count, [anywhere()] * count
    return pl.pallas_call(
        functools.partial(choose_kernel, bits, stacked, len(after)),
        out_shape=out_shape,
        in_specs=[smem()] + [anywhere()] * (2 * count + len(after)),
        out_specs=out_specs,
        scratch_shapes=[pltpu.SemaphoreType.DMA((count,))],
        compiler_params=params(),
        cost_estimate=pl.CostEstimate(flops=SLACK_STRIPES, bytes_accessed=0, transcendentals=0),
        name="stripe_choice",
    )(owners, *carried, *came, *after)


def pack_kernel(first_ref, second_ref, out_ref, sems):
    rows, width = first_ref.shape[0], out_ref.shape[2]
    copies = [pltpu.make_async_copy(second_ref, out_ref.at[1], sems.at[0])]
    for at in range(first_ref.shape[1] // width):
        copies.append(
            pltpu.make_async_copy(
                first_ref.at[:, pl.ds(at * width, width)],
                out_ref.at[0, pl.ds(at * rows, rows)],
                sems.at[1 + at],
            )
        )
    for copy in copies:
        copy.start()
    for copy in copies:
        copy.wait()


def pack(first, second):
    blocks = first.shape[1] // second.shape[1]
    return pl.pallas_call(
        pack_kernel,
        out_shape=jax.ShapeDtypeStruct((2,) + second.shape, second.dtype),
        in_specs=[hbm()] * 2,
        out_specs=hbm(),
        scratch_shapes=[pltpu.SemaphoreType.DMA((1 + blocks,))],
        compiler_params=params(LARGE_LIMIT),
        name="pack_weights",
    )(first, second)


def split_kernel(parts, count, *refs):
    ins, stack_ref, outs, sems = refs[:count], refs[-2 - len(parts)], refs[-1 - len(parts) : -1], refs[-1]
    copies = []
    for out, (at, part) in zip(outs, parts):
        copies.append(pltpu.make_async_copy(ins[at].at[part], out, sems.at[len(copies)]))
    for at in range(count):
        copies.append(pltpu.make_async_copy(ins[at], stack_ref.at[at], sems.at[len(copies)]))
    for copy in copies:
        copy.start()
    for copy in copies:
        copy.wait()


def split(packs, parts, after):
    shape, dtype = packs[0].shape, packs[0].dtype
    stack, *outs = pl.pallas_call(
        functools.partial(split_kernel, parts, len(packs)),
        out_shape=[jax.ShapeDtypeStruct((len(packs),) + shape, dtype)]
        + [jax.ShapeDtypeStruct(shape[1:], dtype)] * len(parts),
        in_specs=[anywhere()] * (len(packs) + len(after)),
        out_specs=[anywhere()] * (1 + len(parts)),
        scratch_shapes=[pltpu.SemaphoreType.DMA((len(parts) + len(packs),))],
        compiler_params=params(),
        cost_estimate=pl.CostEstimate(flops=SLACK_WEIGHTS, bytes_accessed=0, transcendentals=0),
        name="split_packs",
    )(*packs, *after)
    return stack, outs


def tie_kernel(*refs):
    pass


def tie(blocks, after, work=0):
    return pl.pallas_call(
        tie_kernel,
        out_shape=[jax.ShapeDtypeStruct(block.shape, block.dtype) for block in blocks],
        in_specs=[anywhere()] * (len(blocks) + len(after)),
        out_specs=[anywhere()] * len(blocks),
        input_output_aliases={at: at for at in range(len(blocks))},
        compiler_params=params(),
        cost_estimate=pl.CostEstimate(flops=work, bytes_accessed=0, transcendentals=0),
        name="tie",
    )(*blocks, *after)


def prepare_kernel(dense_ref, out_ref):
    out_ref[...] = dense_ref[...].astype(jnp.float32).astype(jnp.bfloat16)


def prepare(dense_weight):
    rows, columns = dense_weight.shape
    step = rows // 4
    return pl.pallas_call(
        prepare_kernel,
        grid=(rows // step,),
        out_shape=jax.ShapeDtypeStruct((rows, columns), jnp.bfloat16),
        in_specs=[pl.BlockSpec((step, columns), lambda i: (i, 0))],
        out_specs=pl.BlockSpec((step, columns), lambda i: (i, 0)),
        compiler_params=params(),
        cost_estimate=pl.CostEstimate(
            flops=2 * rows * columns, bytes_accessed=6 * rows * columns, transcendentals=0
        ),
        name="dense_rows",
    )(dense_weight)


def add_stripes(dense_ref, mine_ref, other_ref, total_ref):
    stripes, half, _ = mine_ref.shape
    core = lax.rem(lax.axis_index("wide"), 2)
    total = None
    for stripe in range(stripes):
        for ref, side in ((mine_ref, core), (other_ref, 1 - core)):
            start = pl.multiple_of((2 * stripe + side) * half, half)
            part = jnp.dot(
                dense_ref[:, pl.ds(start, half)], ref[stripe], preferred_element_type=jnp.float32
            )
            total = part if total is None else total + part
    total_ref[...] = total


def add_blocks(targets_ref, tiles_ref, received_ref, total_ref, count_ref):
    _, parts, block_rows, _ = tiles_ref.shape
    for source in range(parts):
        tile = tiles_ref[0, source].astype(jnp.float32).astype(jnp.bfloat16)
        ones = jnp.ones((tile.shape[1], LANES), jnp.bfloat16)
        weight = jnp.dot(tile, ones, preferred_element_type=jnp.float32)
        for slot in range(received_ref.shape[1] // block_rows):
            block = received_ref[source, pl.ds(slot * block_rows, block_rows), :]
            present = block[0:1, :].astype(jnp.float32) < ABSENT / 2
            product = jnp.dot(tile, block, preferred_element_type=jnp.float32)
            product = jnp.where(present, product, 0.0)
            start = pl.multiple_of(targets_ref[0, slot, source] * block_rows, block_rows)
            total_ref[pl.ds(start, block_rows), :] += product
            count_ref[pl.ds(start, block_rows), :] += jnp.where(present[:, :LANES], weight, 0.0)


def combine(features_ref, total_ref, count_ref, combined_ref):
    scale = lax.rsqrt(count_ref[...])
    for at in range(0, total_ref.shape[1], LANES):
        columns = pl.ds(at, LANES)
        combined_ref[:, columns] = (
            features_ref[:, columns].astype(jnp.float32) + total_ref[:, columns] * scale
        ).astype(jnp.bfloat16)


def place_first(pieces, first_ref):
    me, blocks = lax.axis_index("wide"), first_ref.shape[0]
    for ref, mask in pieces:
        rows = ref.shape[0] // blocks
        start = pl.multiple_of((me ^ mask) * rows, rows)
        for at in range(blocks):
            first_ref[at, pl.ds(start, rows), :] = ref[pl.ds(at * rows, rows), :]


def place_second(pieces, second_ref):
    me = lax.axis_index("wide")
    for ref, mask in pieces:
        rows = ref.shape[0]
        second_ref[pl.ds(pl.multiple_of((me ^ mask) * rows, rows), rows), :] = ref[...]


def rows_kernel(
    targets_ref, dense_ref, mine_ref, other_ref, tiles_ref, received_ref, features_ref, out_ref,
    total_ref, count_ref
):
    ones = jnp.ones((dense_ref.shape[1], LANES), jnp.bfloat16)
    count_ref[...] = 1.0 + jnp.dot(dense_ref[...], ones, preferred_element_type=jnp.float32)
    add_stripes(dense_ref, mine_ref, other_ref, total_ref)
    add_blocks(targets_ref, tiles_ref, received_ref, total_ref, count_ref)
    combine(features_ref, total_ref, count_ref, out_ref)


def combined_rows(targets, dense, mine, other, tiles, received, features):
    return pl.pallas_call(
        rows_kernel,
        out_shape=jax.ShapeDtypeStruct(features.shape, features.dtype),
        in_specs=[smem()] + [vmem()] * 6,
        out_specs=vmem(),
        scratch_shapes=[
            pltpu.VMEM(features.shape, jnp.float32),
            pltpu.VMEM((features.shape[0], LANES), jnp.float32),
        ],
        compiler_params=params(ROWS_LIMIT),
        cost_estimate=pl.CostEstimate(
            flops=ROWS_FLOPS, bytes_accessed=4 * 10**6, transcendentals=0
        ),
        name="combined_rows",
    )(targets, dense, mine, other, tiles, received, features)


def layer_kernel(own, came, late, combined_ref, *refs):
    count = len(own) + len(came) + len(late)
    held = refs[count + 1 : 2 * count + 1]
    out_ref = refs[count]
    first_ref, second_ref, hidden_ref, sems = refs[2 * count + 1 :]
    copies = [
        pltpu.make_async_copy(ref, target, sems.at[at])
        for at, (ref, target) in enumerate(zip(refs[:count], held))
    ]
    for copy in copies:
        copy.start()
    packs = list(zip(held, own))
    for ref, masks in zip(held[len(own) :], came):
        packs += [(ref.at[at], mask) for at, mask in enumerate(masks)]
    pieces = [[(ref.at[which], mask) for ref, mask in packs] for which in range(2)]
    for ref, (which, masks) in zip(held[len(own) + len(came) :], late):
        pieces[which] += [
            (ref if len(masks) == 1 else ref.at[at], mask) for at, mask in enumerate(masks)
        ]
    for copy in copies:
        copy.wait()
    place_first(pieces[0], first_ref)
    width = first_ref.shape[2]
    for at in range(first_ref.shape[0]):
        gated = jnp.dot(combined_ref[...], first_ref[at], preferred_element_type=jnp.float32)
        hidden_ref[:, pl.ds(at * width, width)] = jnp.maximum(gated, 0.0).astype(jnp.bfloat16)
    place_second(pieces[1], second_ref)
    out_ref[...] = jnp.dot(
        hidden_ref[...], second_ref[...], preferred_element_type=jnp.float32
    ).astype(jnp.bfloat16)


def layer(combined, own, came, late, count):
    rows, width = combined.shape
    refs = [block for block, _ in own + came] + [block for block, _, _ in late]
    depth = own[0][0].shape[1] * count
    return pl.pallas_call(
        functools.partial(
            layer_kernel,
            tuple(mask for _, mask in own),
            tuple(masks for _, masks in came),
            tuple((which, masks) for _, which, masks in late),
        ),
        out_shape=jax.ShapeDtypeStruct((rows, width), jnp.bfloat16),
        in_specs=[vmem()] + [anywhere()] * len(refs),
        out_specs=vmem(),
        scratch_shapes=[pltpu.VMEM(ref.shape, ref.dtype) for ref in refs]
        + [
            pltpu.VMEM((depth // width, width, width), jnp.bfloat16),
            pltpu.VMEM((depth, width), jnp.bfloat16),
            pltpu.VMEM((rows, depth), jnp.bfloat16),
            pltpu.SemaphoreType.DMA((len(refs),)),
        ],
        compiler_params=params(LAYER_LIMIT),
        cost_estimate=pl.CostEstimate(
            flops=LAYER_FLOPS, bytes_accessed=LAYER_BYTES, transcendentals=0
        ),
        name="layer",
    )(combined, *refs)


def other_pieces(pieces, wide, order):
    late = {}
    known = [order[0]]
    for bit in order[1:]:
        for mask in known:
            held = late[mask] if mask in late else pieces[mask]
            late[mask ^ bit] = swap(held, wide, bit)
        known = known + [bit] + [mask ^ bit for mask in known]
    return late


def crossed(masks):
    return tuple(mask ^ 1 for mask in masks)


def shards(
    features,
    stripe_owner,
    dense_weight,
    sparse_weight,
    send_blocks,
    target_block,
    first_weight,
    second_weight,
    wide,
    narrow,
):
    block_rows = sparse_weight.shape[2]
    stripes = stripe_owner.shape[1]
    bits = [1 << at for at in range(1, wide.bit_length() - 1)]
    orders = (bits, bits[::-1])
    hops = len(bits)
    owners = jnp.transpose(stripe_owner)
    lists = jnp.transpose(send_blocks, (0, 2, 1))
    targets = jnp.transpose(target_block, (0, 2, 1))

    own = pack(first_weight, second_weight)
    packs = [swap(own, wide, bit) for bit in bits]
    received = lax.all_to_all(pick(lists, features, block_rows), "narrow", 0, 0)

    dense = prepare(dense_weight)

    carried = halves(owners, features, swap(features, wide, 1))
    along = [tuple(orders[k % 2][hop] for k in range(stripes)) for hop in range(hops)]
    came = [swap(block, wide, bit) for block, bit in zip(carried, along[0])]

    own_crossed = swap(own, wide, 1)
    parts = [(bits.index(bit), which) for which in range(2) for bit in orders[which][:-1]]
    stack, forward = split(packs, tuple(parts), [own_crossed] + list(carried))
    ends, end_masks = [], []
    for which in range(2):
        held = {bits[at]: block for (at, of), block in zip(parts, forward) if of == which}
        late = other_pieces(held, wide, orders[which])
        blocks = list(late.values())
        ends.append(blocks[0] if len(blocks) == 1 else jnp.stack(blocks))
        end_masks.append(tuple(late))

    masks = tuple(bits)
    stacks = [(stack, masks), (swap(stack, wide, 1), crossed(masks))]
    for hop in range(1, hops):
        carried = choose(owners, along[hop - 1], carried, came, False, [dense, stack])
        came = [swap(block, wide, bit) for block, bit in zip(carried, along[hop])]
    carried = choose(owners, along[-1], carried, came, True, ends)
    other = swap(carried, wide, 1)
    ends = tie(ends, [stacks[1][0]])

    crossed_ends = [swap(end, wide, 1) for end in ends]
    late = []
    for which in range(2):
        late.append((ends[which], which, end_masks[which]))
        late.append((crossed_ends[which], which, crossed(end_masks[which])))

    combined = combined_rows(
        targets, dense, carried, other, sparse_weight, received, features
    )
    return layer(combined, [(own, 0), (own_crossed, 1)], stacks, late, wide)


def solution(mesh):
    placed = (
        P(("wide", "narrow"), None),
        P(),
        P(("wide", "narrow"), None),
        P(("wide", "narrow"), None, None, None),
        P(("wide", "narrow"), None, None),
        P(("wide", "narrow"), None, None),
        P("wide", None),
        P("wide", None),
    )
    local = functools.partial(shards, wide=mesh.shape["wide"], narrow=mesh.shape["narrow"])
    return jax.shard_map(
        local, mesh=mesh, in_specs=placed, out_specs=P(("wide", "narrow"), None), check_vma=False
    )
```

```python
import functools

import jax
import jax.numpy as jnp
from jax import lax
from jax.experimental import pallas as pl
from jax.experimental.pallas import tpu as pltpu
from jax.sharding import PartitionSpec as P

LANES = 128
ABSENT = 64.0
VMEM_LIMIT = 48 * 1024 * 1024
LARGE_LIMIT = 48 * 1024 * 1024
SLACK_WEIGHTS = 2 * 10**9
ROWS_FLOPS = 0
ROWS_LIMIT = 48 * 2**20
LAYER_FLOPS = 10**11
LAYER_BYTES = 4 * 10**6
LAYER_LIMIT = 48 * 2**20
SLACK_STRIPES = 2 * 10**9


def params(limit=VMEM_LIMIT):
    return pltpu.CompilerParams(vmem_limit_bytes=limit)


def vmem():
    return pl.BlockSpec(memory_space=pltpu.VMEM)


def smem():
    return pl.BlockSpec(memory_space=pltpu.SMEM)


def anywhere():
    return pl.BlockSpec(memory_space=pl.ANY)


def hbm():
    return pl.BlockSpec(memory_space=pltpu.HBM)


def swap(block, count, bit):
    return lax.ppermute(block, "wide", [(i, i ^ bit) for i in range(count)])


def pick_kernel(parts, cap, block_rows, lists_ref, features_ref, out_ref, empty_ref, sems):
    empty_ref[...] = jnp.full(empty_ref.shape, ABSENT, empty_ref.dtype)
    copies = []
    for to in range(parts):
        for slot in range(cap):
            listed = lists_ref[0, slot, to]
            target = out_ref.at[to, pl.ds(slot * block_rows, block_rows)]
            sem = sems.at[len(copies)]
            start = pl.multiple_of(jnp.maximum(listed, 0) * block_rows, block_rows)
            real = pltpu.make_async_copy(features_ref.at[pl.ds(start, block_rows)], target, sem)
            blank = pltpu.make_async_copy(empty_ref, target, sem)

            @pl.when(listed >= 0)
            def _():
                real.start()

            @pl.when(listed < 0)
            def _():
                blank.start()

            copies.append(blank)
    for copy in copies:
        copy.wait()


def pick(lists, features, block_rows):
    _, cap, parts = lists.shape
    width = features.shape[1]
    return pl.pallas_call(
        functools.partial(pick_kernel, parts, cap, block_rows),
        out_shape=jax.ShapeDtypeStruct((parts, cap * block_rows, width), features.dtype),
        in_specs=[smem(), hbm()],
        out_specs=hbm(),
        scratch_shapes=[
            pltpu.VMEM((block_rows, width), features.dtype),
            pltpu.SemaphoreType.DMA((parts * cap,)),
        ],
        compiler_params=params(LARGE_LIMIT),
        name="pick_blocks",
    )(lists, features)


def halves_kernel(owners_ref, mine_ref, other_ref, *rest):
    outs, sems = rest[:-1], rest[-1]
    core, part = lax.rem(lax.axis_index("wide"), 2), lax.axis_index("narrow")
    half = outs[0].shape[0]
    rows = pl.ds(pl.multiple_of(core * half, half), half)
    copies = []
    for k, out in enumerate(outs):
        own = (owners_ref[k, part] & 1) == core
        kept = pltpu.make_async_copy(mine_ref.at[rows], out, sems.at[k])
        came = pltpu.make_async_copy(other_ref.at[rows], out, sems.at[k])

        @pl.when(own)
        def _():
            kept.start()

        @pl.when(jnp.logical_not(own))
        def _():
            came.start()

        copies.append(kept)
    for copy in copies:
        copy.wait()


def halves(owners, mine, other):
    rows, width = mine.shape
    stripes = owners.shape[0]
    return pl.pallas_call(
        halves_kernel,
        out_shape=[jax.ShapeDtypeStruct((rows // 2, width), mine.dtype)] * stripes,
        in_specs=[smem(), anywhere(), anywhere()],
        out_specs=[anywhere()] * stripes,
        scratch_shapes=[pltpu.SemaphoreType.DMA((stripes,))],
        compiler_params=params(),
        name="stripe_halves",
    )(owners, mine, other)


def choose_kernel(bits, stacked, others, owners_ref, *refs):
    count = len(bits)
    refs = refs[: 2 * count] + refs[2 * count + others :]
    sems = refs[-1]
    me, part = lax.axis_index("wide"), lax.axis_index("narrow")
    copies = []
    for k, bit in enumerate(bits):
        out = refs[2 * count].at[k] if stacked else refs[2 * count + k]
        same = ((owners_ref[k, part] ^ me) & bit) == 0
        kept = pltpu.make_async_copy(refs[k], out, sems.at[k])
        came = pltpu.make_async_copy(refs[count + k], out, sems.at[k])

        @pl.when(same)
        def _():
            kept.start()

        @pl.when(jnp.logical_not(same))
        def _():
            came.start()

        copies.append(kept)
    for copy in copies:
        copy.wait()


def choose(owners, bits, carried, came, stacked, after):
    count = len(bits)
    shape, dtype = carried[0].shape, carried[0].dtype
    if stacked:
        out_shape, out_specs = jax.ShapeDtypeStruct((count,) + shape, dtype), anywhere()
    else:
        out_shape, out_specs = [jax.ShapeDtypeStruct(shape, dtype)] * count, [anywhere()] * count
    return pl.pallas_call(
        functools.partial(choose_kernel, bits, stacked, len(after)),
        out_shape=out_shape,
        in_specs=[smem()] + [anywhere()] * (2 * count + len(after)),
        out_specs=out_specs,
        scratch_shapes=[pltpu.SemaphoreType.DMA((count,))],
        compiler_params=params(),
        cost_estimate=pl.CostEstimate(flops=SLACK_STRIPES, bytes_accessed=0, transcendentals=0),
        name="stripe_choice",
    )(owners, *carried, *came, *after)


def join_kernel(sizes, *refs):
    count = sum(sizes)
    sems, outs = refs[-1], refs[count:-1]
    copies, at = [], 0
    for out, size in zip(outs, sizes):
        for place in range(size):
            copies.append(pltpu.make_async_copy(refs[at], out.at[place], sems.at[at]))
            at += 1
    for copy in copies:
        copy.start()
    for copy in copies:
        copy.wait()


def join(stacks):
    flat = [piece for stack in stacks for piece in stack]
    sizes = tuple(len(stack) for stack in stacks)
    return pl.pallas_call(
        functools.partial(join_kernel, sizes),
        out_shape=[
            jax.ShapeDtypeStruct((len(stack),) + stack[0].shape, stack[0].dtype) for stack in stacks
        ],
        in_specs=[anywhere()] * len(flat),
        out_specs=[anywhere()] * len(stacks),
        scratch_shapes=[pltpu.SemaphoreType.DMA((len(flat),))],
        compiler_params=params(),
        cost_estimate=pl.CostEstimate(flops=SLACK_WEIGHTS, bytes_accessed=0, transcendentals=0),
        name="join_pieces",
    )(*flat)


def tie_kernel(*refs):
    pass


def tie(blocks, after, work=0):
    return pl.pallas_call(
        tie_kernel,
        out_shape=[jax.ShapeDtypeStruct(block.shape, block.dtype) for block in blocks],
        in_specs=[anywhere()] * (len(blocks) + len(after)),
        out_specs=[anywhere()] * len(blocks),
        input_output_aliases={at: at for at in range(len(blocks))},
        compiler_params=params(),
        cost_estimate=pl.CostEstimate(flops=work, bytes_accessed=0, transcendentals=0),
        name="tie",
    )(*blocks, *after)


def prepare_kernel(dense_ref, out_ref):
    out_ref[...] = dense_ref[...].astype(jnp.float32).astype(jnp.bfloat16)


def prepare(dense_weight):
    rows, columns = dense_weight.shape
    step = rows // 4
    return pl.pallas_call(
        prepare_kernel,
        grid=(rows // step,),
        out_shape=jax.ShapeDtypeStruct((rows, columns), jnp.bfloat16),
        in_specs=[pl.BlockSpec((step, columns), lambda i: (i, 0))],
        out_specs=pl.BlockSpec((step, columns), lambda i: (i, 0)),
        compiler_params=params(),
        cost_estimate=pl.CostEstimate(
            flops=2 * rows * columns, bytes_accessed=6 * rows * columns, transcendentals=0
        ),
        name="dense_rows",
    )(dense_weight)


def add_stripes(dense_ref, mine_ref, other_ref, total_ref):
    stripes, half, _ = mine_ref.shape
    core = lax.rem(lax.axis_index("wide"), 2)
    total = None
    for stripe in range(stripes):
        for ref, side in ((mine_ref, core), (other_ref, 1 - core)):
            start = pl.multiple_of((2 * stripe + side) * half, half)
            part = jnp.dot(
                dense_ref[:, pl.ds(start, half)], ref[stripe], preferred_element_type=jnp.float32
            )
            total = part if total is None else total + part
    total_ref[...] = total


def add_blocks(targets_ref, tiles_ref, received_ref, total_ref, count_ref):
    _, parts, block_rows, _ = tiles_ref.shape
    for source in range(parts):
        tile = tiles_ref[0, source].astype(jnp.float32).astype(jnp.bfloat16)
        ones = jnp.ones((tile.shape[1], LANES), jnp.bfloat16)
        weight = jnp.dot(tile, ones, preferred_element_type=jnp.float32)
        for slot in range(received_ref.shape[1] // block_rows):
            block = received_ref[source, pl.ds(slot * block_rows, block_rows), :]
            present = block[0:1, :].astype(jnp.float32) < ABSENT / 2
            product = jnp.dot(tile, block, preferred_element_type=jnp.float32)
            product = jnp.where(present, product, 0.0)
            start = pl.multiple_of(targets_ref[0, slot, source] * block_rows, block_rows)
            total_ref[pl.ds(start, block_rows), :] += product
            count_ref[pl.ds(start, block_rows), :] += jnp.where(present[:, :LANES], weight, 0.0)


def combine(features_ref, total_ref, more_ref, count_ref, combined_ref):
    scale = lax.rsqrt(count_ref[...])
    for at in range(0, total_ref.shape[1], LANES):
        columns = pl.ds(at, LANES)
        combined_ref[:, columns] = (
            features_ref[:, columns].astype(jnp.float32)
            + (total_ref[:, columns] + more_ref[:, columns]) * scale
        ).astype(jnp.bfloat16)


def place_first(pieces, first_ref):
    me, (blocks, _, width) = lax.axis_index("wide"), first_ref.shape
    for ref, mask in pieces:
        rows = ref.shape[0]
        start = pl.multiple_of((me ^ mask) * rows, rows)
        for at in range(blocks):
            first_ref[at, pl.ds(start, rows), :] = ref[:, pl.ds(at * width, width)]


def place_second(pieces, second_ref):
    me = lax.axis_index("wide")
    for ref, mask in pieces:
        rows = ref.shape[0]
        second_ref[pl.ds(pl.multiple_of((me ^ mask) * rows, rows), rows), :] = ref[...]


def blocks_kernel(targets_ref, tiles_ref, received_ref, total_ref, count_ref):
    total_ref[...] = jnp.zeros_like(total_ref)
    count_ref[...] = jnp.ones_like(count_ref)
    add_blocks(targets_ref, tiles_ref, received_ref, total_ref, count_ref)


def block_sums(targets, tiles, received, rows):
    width = received.shape[2]
    return pl.pallas_call(
        blocks_kernel,
        out_shape=[
            jax.ShapeDtypeStruct((rows, width), jnp.float32),
            jax.ShapeDtypeStruct((rows, LANES), jnp.float32),
        ],
        in_specs=[smem(), vmem(), vmem()],
        out_specs=[vmem(), vmem()],
        compiler_params=params(ROWS_LIMIT),
        cost_estimate=pl.CostEstimate(
            flops=ROWS_FLOPS, bytes_accessed=2 * 10**6, transcendentals=0
        ),
        name="block_sums",
    )(targets, tiles, received)


def rows_kernel(
    dense_ref, mine_ref, other_ref, total_ref, count_ref, features_ref, out_ref, sum_ref, degree_ref
):
    ones = jnp.ones((dense_ref.shape[1], LANES), jnp.bfloat16)
    degree_ref[...] = count_ref[...] + jnp.dot(
        dense_ref[...], ones, preferred_element_type=jnp.float32
    )
    add_stripes(dense_ref, mine_ref, other_ref, sum_ref)
    combine(features_ref, sum_ref, total_ref, degree_ref, out_ref)


def combined_rows(dense, mine, other, total, count, features):
    return pl.pallas_call(
        rows_kernel,
        out_shape=jax.ShapeDtypeStruct(features.shape, features.dtype),
        in_specs=[vmem()] * 6,
        out_specs=vmem(),
        scratch_shapes=[
            pltpu.VMEM(features.shape, jnp.float32),
            pltpu.VMEM((features.shape[0], LANES), jnp.float32),
        ],
        compiler_params=params(ROWS_LIMIT),
        cost_estimate=pl.CostEstimate(
            flops=ROWS_FLOPS, bytes_accessed=4 * 10**6, transcendentals=0
        ),
        name="combined_rows",
    )(dense, mine, other, total, count, features)


def layer_kernel(parts, combined_ref, *refs):
    count = len(parts)
    out_ref, held = refs[count], refs[count + 1 : 2 * count + 1]
    first_ref, second_ref, hidden_ref, sems = refs[2 * count + 1 :]
    copies = [
        pltpu.make_async_copy(ref, target, sems.at[at])
        for at, (ref, target) in enumerate(zip(refs[:count], held))
    ]
    for copy in copies:
        copy.start()
    pieces = ([], [])
    for ref, (which, masks) in zip(held, parts):
        pieces[which].extend(
            (ref if len(ref.shape) == 2 else ref.at[at], mask) for at, mask in enumerate(masks)
        )
    for copy in copies:
        copy.wait()
    place_first(pieces[0], first_ref)
    width = first_ref.shape[2]
    for at in range(first_ref.shape[0]):
        gated = jnp.dot(combined_ref[...], first_ref[at], preferred_element_type=jnp.float32)
        hidden_ref[:, pl.ds(at * width, width)] = jnp.maximum(gated, 0.0).astype(jnp.bfloat16)
    place_second(pieces[1], second_ref)
    out_ref[...] = jnp.dot(
        hidden_ref[...], second_ref[...], preferred_element_type=jnp.float32
    ).astype(jnp.bfloat16)


def layer(combined, parts, depth):
    rows, width = combined.shape
    refs = [block for block, _, _ in parts]
    return pl.pallas_call(
        functools.partial(layer_kernel, tuple((which, masks) for _, which, masks in parts)),
        out_shape=jax.ShapeDtypeStruct((rows, width), jnp.bfloat16),
        in_specs=[vmem()] + [anywhere()] * len(refs),
        out_specs=vmem(),
        scratch_shapes=[pltpu.VMEM(ref.shape, ref.dtype) for ref in refs]
        + [
            pltpu.VMEM((depth // width, width, width), jnp.bfloat16),
            pltpu.VMEM((depth, width), jnp.bfloat16),
            pltpu.VMEM((rows, depth), jnp.bfloat16),
            pltpu.SemaphoreType.DMA((len(refs),)),
        ],
        compiler_params=params(LAYER_LIMIT),
        cost_estimate=pl.CostEstimate(
            flops=LAYER_FLOPS, bytes_accessed=LAYER_BYTES, transcendentals=0
        ),
        name="layer",
    )(combined, *refs)


def other_pieces(pieces, wide, order):
    late = {}
    known = [order[0]]
    for bit in order[1:]:
        for mask in known:
            held = late[mask] if mask in late else pieces[mask]
            late[mask ^ bit] = swap(held, wide, bit)
        known = known + [bit] + [mask ^ bit for mask in known]
    return late


def crossed(masks):
    return tuple(mask ^ 1 for mask in masks)


def shards(
    features,
    stripe_owner,
    dense_weight,
    sparse_weight,
    send_blocks,
    target_block,
    first_weight,
    second_weight,
    wide,
    narrow,
):
    block_rows = sparse_weight.shape[2]
    stripes = stripe_owner.shape[1]
    bits = [1 << at for at in range(1, wide.bit_length() - 1)]
    orders = (bits, bits[::-1])
    hops = len(bits)
    owners = jnp.transpose(stripe_owner)
    lists = jnp.transpose(send_blocks, (0, 2, 1))
    targets = jnp.transpose(target_block, (0, 2, 1))

    pieces = []
    for shard in (first_weight, second_weight):
        held = {0: shard}
        for bit in bits:
            held[bit] = swap(shard, wide, bit)
        pieces.append(held)
    received = lax.all_to_all(pick(lists, features, block_rows), "narrow", 0, 0)

    dense = prepare(dense_weight)

    carried = halves(owners, features, swap(features, wide, 1))
    along = [tuple(orders[k % 2][hop] for k in range(stripes)) for hop in range(hops)]
    came = [swap(block, wide, bit) for block, bit in zip(carried, along[0])]

    stacks = join([list(held.values()) for held in pieces])
    crossed_stacks = [swap(stack, wide, 1) for stack in stacks]
    masks = (0,) + tuple(bits)
    ends, end_masks = [], []
    for held, order in zip(pieces, orders):
        late = other_pieces(held, wide, order)
        blocks = list(late.values())
        ends.append(blocks[0] if len(blocks) == 1 else jnp.stack(blocks))
        end_masks.append(tuple(late))

    for hop in range(1, hops):
        carried = choose(owners, along[hop - 1], carried, came, False, [dense, stacks[0]])
        came = [swap(block, wide, bit) for block, bit in zip(carried, along[hop])]
    carried = choose(owners, along[-1], carried, came, True, ends)
    other = swap(carried, wide, 1)
    ends = tie(ends, crossed_stacks)
    parts = []
    for which in range(2):
        parts.append((stacks[which], which, masks))
        parts.append((crossed_stacks[which], which, crossed(masks)))
        parts.append((ends[which], which, end_masks[which]))
        parts.append((swap(ends[which], wide, 1), which, crossed(end_masks[which])))

    total, count = block_sums(targets, sparse_weight, received, features.shape[0])
    combined = combined_rows(dense, carried, other, total, count, features)
    return layer(combined, parts, second_weight.shape[0] * wide)


def solution(mesh):
    placed = (
        P(("wide", "narrow"), None),
        P(),
        P(("wide", "narrow"), None),
        P(("wide", "narrow"), None, None, None),
        P(("wide", "narrow"), None, None),
        P(("wide", "narrow"), None, None),
        P("wide", None),
        P("wide", None),
    )
    local = functools.partial(shards, wide=mesh.shape["wide"], narrow=mesh.shape["narrow"])
    return jax.shard_map(
        local, mesh=mesh, in_specs=placed, out_specs=P(("wide", "narrow"), None), check_vma=False
    )
```

```python
import functools

import jax
import jax.numpy as jnp
from jax import lax
from jax.experimental import pallas as pl
from jax.experimental.pallas import tpu as pltpu
from jax.sharding import PartitionSpec as P

LANES = 128
ABSENT = 64.0
VMEM_LIMIT = 48 * 1024 * 1024
LARGE_LIMIT = 48 * 1024 * 1024
SLACK_WEIGHTS = 2 * 10**9
ROWS_FLOPS = 0
ROWS_LIMIT = 48 * 2**20
LAYER_FLOPS = 10**11
LAYER_BYTES = 4 * 10**6
LAYER_LIMIT = 48 * 2**20
SLACK_STRIPES = 2 * 10**9


def params(limit=VMEM_LIMIT):
    return pltpu.CompilerParams(vmem_limit_bytes=limit)


def vmem():
    return pl.BlockSpec(memory_space=pltpu.VMEM)


def smem():
    return pl.BlockSpec(memory_space=pltpu.SMEM)


def anywhere():
    return pl.BlockSpec(memory_space=pl.ANY)


def hbm():
    return pl.BlockSpec(memory_space=pltpu.HBM)


def swap(block, count, bit):
    return lax.ppermute(block, "wide", [(i, i ^ bit) for i in range(count)])


def pick_kernel(parts, cap, block_rows, lists_ref, features_ref, out_ref, empty_ref, sems):
    empty_ref[...] = jnp.full(empty_ref.shape, ABSENT, empty_ref.dtype)
    copies = []
    for to in range(parts):
        for slot in range(cap):
            listed = lists_ref[0, slot, to]
            target = out_ref.at[to, pl.ds(slot * block_rows, block_rows)]
            sem = sems.at[len(copies)]
            start = pl.multiple_of(jnp.maximum(listed, 0) * block_rows, block_rows)
            real = pltpu.make_async_copy(features_ref.at[pl.ds(start, block_rows)], target, sem)
            blank = pltpu.make_async_copy(empty_ref, target, sem)

            @pl.when(listed >= 0)
            def _():
                real.start()

            @pl.when(listed < 0)
            def _():
                blank.start()

            copies.append(blank)
    for copy in copies:
        copy.wait()


def pick(lists, features, block_rows):
    _, cap, parts = lists.shape
    width = features.shape[1]
    return pl.pallas_call(
        functools.partial(pick_kernel, parts, cap, block_rows),
        out_shape=jax.ShapeDtypeStruct((parts, cap * block_rows, width), features.dtype),
        in_specs=[smem(), hbm()],
        out_specs=hbm(),
        scratch_shapes=[
            pltpu.VMEM((block_rows, width), features.dtype),
            pltpu.SemaphoreType.DMA((parts * cap,)),
        ],
        compiler_params=params(LARGE_LIMIT),
        name="pick_blocks",
    )(lists, features)


def halves_kernel(owners_ref, mine_ref, other_ref, *rest):
    outs, sems = rest[:-1], rest[-1]
    core, part = lax.rem(lax.axis_index("wide"), 2), lax.axis_index("narrow")
    half = outs[0].shape[0]
    rows = pl.ds(pl.multiple_of(core * half, half), half)
    copies = []
    for k, out in enumerate(outs):
        own = (owners_ref[k, part] & 1) == core
        kept = pltpu.make_async_copy(mine_ref.at[rows], out, sems.at[k])
        came = pltpu.make_async_copy(other_ref.at[rows], out, sems.at[k])

        @pl.when(own)
        def _():
            kept.start()

        @pl.when(jnp.logical_not(own))
        def _():
            came.start()

        copies.append(kept)
    for copy in copies:
        copy.wait()


def halves(owners, mine, other):
    rows, width = mine.shape
    stripes = owners.shape[0]
    return pl.pallas_call(
        halves_kernel,
        out_shape=[jax.ShapeDtypeStruct((rows // 2, width), mine.dtype)] * stripes,
        in_specs=[smem(), anywhere(), anywhere()],
        out_specs=[anywhere()] * stripes,
        scratch_shapes=[pltpu.SemaphoreType.DMA((stripes,))],
        compiler_params=params(),
        name="stripe_halves",
    )(owners, mine, other)


def choose_kernel(bits, stacked, others, owners_ref, *refs):
    count = len(bits)
    refs = refs[: 2 * count] + refs[2 * count + others :]
    sems = refs[-1]
    me, part = lax.axis_index("wide"), lax.axis_index("narrow")
    copies = []
    for k, bit in enumerate(bits):
        out = refs[2 * count].at[k] if stacked else refs[2 * count + k]
        same = ((owners_ref[k, part] ^ me) & bit) == 0
        kept = pltpu.make_async_copy(refs[k], out, sems.at[k])
        came = pltpu.make_async_copy(refs[count + k], out, sems.at[k])

        @pl.when(same)
        def _():
            kept.start()

        @pl.when(jnp.logical_not(same))
        def _():
            came.start()

        copies.append(kept)
    for copy in copies:
        copy.wait()


def choose(owners, bits, carried, came, stacked, after):
    count = len(bits)
    shape, dtype = carried[0].shape, carried[0].dtype
    if stacked:
        out_shape, out_specs = jax.ShapeDtypeStruct((count,) + shape, dtype), anywhere()
    else:
        out_shape, out_specs = [jax.ShapeDtypeStruct(shape, dtype)] * count, [anywhere()] * count
    return pl.pallas_call(
        functools.partial(choose_kernel, bits, stacked, len(after)),
        out_shape=out_shape,
        in_specs=[smem()] + [anywhere()] * (2 * count + len(after)),
        out_specs=out_specs,
        scratch_shapes=[pltpu.SemaphoreType.DMA((count,))],
        compiler_params=params(),
        cost_estimate=pl.CostEstimate(flops=SLACK_STRIPES, bytes_accessed=0, transcendentals=0),
        name="stripe_choice",
    )(owners, *carried, *came, *after)


def join_kernel(sizes, *refs):
    count = sum(sizes)
    sems, outs = refs[-1], refs[count:-1]
    copies, at = [], 0
    for out, size in zip(outs, sizes):
        for place in range(size):
            copies.append(pltpu.make_async_copy(refs[at], out.at[place], sems.at[at]))
            at += 1
    for copy in copies:
        copy.start()
    for copy in copies:
        copy.wait()


def join(stacks):
    flat = [piece for stack in stacks for piece in stack]
    sizes = tuple(len(stack) for stack in stacks)
    return pl.pallas_call(
        functools.partial(join_kernel, sizes),
        out_shape=[
            jax.ShapeDtypeStruct((len(stack),) + stack[0].shape, stack[0].dtype) for stack in stacks
        ],
        in_specs=[anywhere()] * len(flat),
        out_specs=[anywhere()] * len(stacks),
        scratch_shapes=[pltpu.SemaphoreType.DMA((len(flat),))],
        compiler_params=params(),
        cost_estimate=pl.CostEstimate(flops=SLACK_WEIGHTS, bytes_accessed=0, transcendentals=0),
        name="join_pieces",
    )(*flat)


def tie_kernel(*refs):
    pass


def tie(blocks, after, work=0):
    return pl.pallas_call(
        tie_kernel,
        out_shape=[jax.ShapeDtypeStruct(block.shape, block.dtype) for block in blocks],
        in_specs=[anywhere()] * (len(blocks) + len(after)),
        out_specs=[anywhere()] * len(blocks),
        input_output_aliases={at: at for at in range(len(blocks))},
        compiler_params=params(),
        cost_estimate=pl.CostEstimate(flops=work, bytes_accessed=0, transcendentals=0),
        name="tie",
    )(*blocks, *after)


def prepare_kernel(dense_ref, tiles_ref, out_ref, tiles_out):
    out_ref[...] = dense_ref[...].astype(jnp.float32).astype(jnp.bfloat16)
    tiles_out[...] = tiles_ref[...].astype(jnp.float32).astype(jnp.bfloat16)


def prepare(dense_weight, tiles):
    rows, columns = dense_weight.shape
    step = rows // 4
    return pl.pallas_call(
        prepare_kernel,
        grid=(rows // step,),
        out_shape=[
            jax.ShapeDtypeStruct((rows, columns), jnp.bfloat16),
            jax.ShapeDtypeStruct(tiles.shape, jnp.bfloat16),
        ],
        in_specs=[
            pl.BlockSpec((step, columns), lambda i: (i, 0)),
            pl.BlockSpec(tiles.shape, lambda i: (0, 0, 0, 0)),
        ],
        out_specs=[
            pl.BlockSpec((step, columns), lambda i: (i, 0)),
            pl.BlockSpec(tiles.shape, lambda i: (0, 0, 0, 0)),
        ],
        compiler_params=params(),
        cost_estimate=pl.CostEstimate(
            flops=2 * rows * columns, bytes_accessed=6 * rows * columns, transcendentals=0
        ),
        name="dense_rows",
    )(dense_weight, tiles)


def add_stripes(dense_ref, mine_ref, other_ref, total_ref):
    stripes, half, _ = mine_ref.shape
    core = lax.rem(lax.axis_index("wide"), 2)
    total = None
    for stripe in range(stripes):
        for ref, side in ((mine_ref, core), (other_ref, 1 - core)):
            start = pl.multiple_of((2 * stripe + side) * half, half)
            part = jnp.dot(
                dense_ref[:, pl.ds(start, half)], ref[stripe], preferred_element_type=jnp.float32
            )
            total = part if total is None else total + part
    total_ref[...] = total


def add_blocks(targets_ref, tiles_ref, received_ref, total_ref, count_ref):
    _, parts, block_rows, _ = tiles_ref.shape
    for source in range(parts):
        tile = tiles_ref[0, source]
        ones = jnp.ones((tile.shape[1], LANES), jnp.bfloat16)
        weight = jnp.dot(tile, ones, preferred_element_type=jnp.float32)
        for slot in range(received_ref.shape[1] // block_rows):
            block = received_ref[source, pl.ds(slot * block_rows, block_rows), :]
            present = block[0:1, :].astype(jnp.float32) < ABSENT / 2
            product = jnp.dot(tile, block, preferred_element_type=jnp.float32)
            product = jnp.where(present, product, 0.0)
            start = pl.multiple_of(targets_ref[0, slot, source] * block_rows, block_rows)
            total_ref[pl.ds(start, block_rows), :] += product
            count_ref[pl.ds(start, block_rows), :] += jnp.where(present[:, :LANES], weight, 0.0)


def combine(features_ref, total_ref, more_ref, count_ref, combined_ref):
    scale = lax.rsqrt(count_ref[...])
    for at in range(0, total_ref.shape[1], LANES):
        columns = pl.ds(at, LANES)
        combined_ref[:, columns] = (
            features_ref[:, columns].astype(jnp.float32)
            + (total_ref[:, columns] + more_ref[:, columns]) * scale
        ).astype(jnp.bfloat16)


def place_first(pieces, first_ref):
    me, (blocks, _, width) = lax.axis_index("wide"), first_ref.shape
    for ref, mask in pieces:
        rows = ref.shape[0]
        start = pl.multiple_of((me ^ mask) * rows, rows)
        for at in range(blocks):
            first_ref[at, pl.ds(start, rows), :] = ref[:, pl.ds(at * width, width)]


def place_second(pieces, second_ref):
    me = lax.axis_index("wide")
    for ref, mask in pieces:
        rows = ref.shape[0]
        second_ref[pl.ds(pl.multiple_of((me ^ mask) * rows, rows), rows), :] = ref[...]


def blocks_kernel(targets_ref, tiles_ref, received_ref, total_ref, count_ref):
    total_ref[...] = jnp.zeros_like(total_ref)
    count_ref[...] = jnp.ones_like(count_ref)
    add_blocks(targets_ref, tiles_ref, received_ref, total_ref, count_ref)


def block_sums(targets, tiles, received, rows):
    width = received.shape[2]
    return pl.pallas_call(
        blocks_kernel,
        out_shape=[
            jax.ShapeDtypeStruct((rows, width), jnp.float32),
            jax.ShapeDtypeStruct((rows, LANES), jnp.float32),
        ],
        in_specs=[smem(), vmem(), vmem()],
        out_specs=[vmem(), vmem()],
        compiler_params=params(ROWS_LIMIT),
        cost_estimate=pl.CostEstimate(
            flops=ROWS_FLOPS, bytes_accessed=2 * 10**6, transcendentals=0
        ),
        name="block_sums",
    )(targets, tiles, received)


def rows_kernel(
    dense_ref, mine_ref, other_ref, total_ref, count_ref, features_ref, out_ref, sum_ref, degree_ref
):
    ones = jnp.ones((dense_ref.shape[1], LANES), jnp.bfloat16)
    degree_ref[...] = count_ref[...] + jnp.dot(
        dense_ref[...], ones, preferred_element_type=jnp.float32
    )
    add_stripes(dense_ref, mine_ref, other_ref, sum_ref)
    combine(features_ref, sum_ref, total_ref, degree_ref, out_ref)


def combined_rows(dense, mine, other, total, count, features):
    return pl.pallas_call(
        rows_kernel,
        out_shape=jax.ShapeDtypeStruct(features.shape, features.dtype),
        in_specs=[vmem()] * 6,
        out_specs=vmem(),
        scratch_shapes=[
            pltpu.VMEM(features.shape, jnp.float32),
            pltpu.VMEM((features.shape[0], LANES), jnp.float32),
        ],
        compiler_params=params(ROWS_LIMIT),
        cost_estimate=pl.CostEstimate(
            flops=ROWS_FLOPS, bytes_accessed=4 * 10**6, transcendentals=0
        ),
        name="combined_rows",
    )(dense, mine, other, total, count, features)


def layer_kernel(parts, combined_ref, *refs):
    count = len(parts)
    out_ref, held = refs[count], refs[count + 1 : 2 * count + 1]
    first_ref, second_ref, hidden_ref, sems = refs[2 * count + 1 :]
    copies = [
        pltpu.make_async_copy(ref, target, sems.at[at])
        for at, (ref, target) in enumerate(zip(refs[:count], held))
    ]
    for copy in copies:
        copy.start()
    pieces = ([], [])
    for ref, (which, masks) in zip(held, parts):
        pieces[which].extend(
            (ref if len(ref.shape) == 2 else ref.at[at], mask) for at, mask in enumerate(masks)
        )
    for copy, (which, _) in zip(copies, parts):
        if which == 0:
            copy.wait()
    place_first(pieces[0], first_ref)
    width = first_ref.shape[2]
    for at in range(first_ref.shape[0]):
        gated = jnp.dot(combined_ref[...], first_ref[at], preferred_element_type=jnp.float32)
        hidden_ref[:, pl.ds(at * width, width)] = jnp.maximum(gated, 0.0).astype(jnp.bfloat16)
    for copy, (which, _) in zip(copies, parts):
        if which == 1:
            copy.wait()
    place_second(pieces[1], second_ref)
    out_ref[...] = jnp.dot(
        hidden_ref[...], second_ref[...], preferred_element_type=jnp.float32
    ).astype(jnp.bfloat16)


def layer(combined, parts, depth):
    rows, width = combined.shape
    refs = [block for block, _, _ in parts]
    return pl.pallas_call(
        functools.partial(layer_kernel, tuple((which, masks) for _, which, masks in parts)),
        out_shape=jax.ShapeDtypeStruct((rows, width), jnp.bfloat16),
        in_specs=[vmem()] + [anywhere()] * len(refs),
        out_specs=vmem(),
        scratch_shapes=[pltpu.VMEM(ref.shape, ref.dtype) for ref in refs]
        + [
            pltpu.VMEM((depth // width, width, width), jnp.bfloat16),
            pltpu.VMEM((depth, width), jnp.bfloat16),
            pltpu.VMEM((rows, depth), jnp.bfloat16),
            pltpu.SemaphoreType.DMA((len(refs),)),
        ],
        compiler_params=params(LAYER_LIMIT),
        cost_estimate=pl.CostEstimate(
            flops=LAYER_FLOPS, bytes_accessed=LAYER_BYTES, transcendentals=0
        ),
        name="layer",
    )(combined, *refs)


def other_pieces(pieces, wide, order):
    late = {}
    known = [order[0]]
    for bit in order[1:]:
        for mask in known:
            held = late[mask] if mask in late else pieces[mask]
            late[mask ^ bit] = swap(held, wide, bit)
        known = known + [bit] + [mask ^ bit for mask in known]
    return late


def crossed(masks):
    return tuple(mask ^ 1 for mask in masks)


def shards(
    features,
    stripe_owner,
    dense_weight,
    sparse_weight,
    send_blocks,
    target_block,
    first_weight,
    second_weight,
    wide,
    narrow,
):
    block_rows = sparse_weight.shape[2]
    stripes = stripe_owner.shape[1]
    bits = [1 << at for at in range(1, wide.bit_length() - 1)]
    orders = (bits, bits[::-1])
    hops = len(bits)
    owners = jnp.transpose(stripe_owner)
    lists = jnp.transpose(send_blocks, (0, 2, 1))
    targets = jnp.transpose(target_block, (0, 2, 1))

    pieces = []
    for shard in (first_weight, second_weight):
        held = {0: shard}
        for bit in bits:
            held[bit] = swap(shard, wide, bit)
        pieces.append(held)
    received = lax.all_to_all(pick(lists, features, block_rows), "narrow", 0, 0)

    dense, tiles = prepare(dense_weight, sparse_weight)

    carried = halves(owners, features, swap(features, wide, 1))
    along = [tuple(orders[k % 2][hop] for k in range(stripes)) for hop in range(hops)]
    came = [swap(block, wide, bit) for block, bit in zip(carried, along[0])]

    stacks = join([list(held.values()) for held in pieces])
    crossed_stacks = [swap(stack, wide, 1) for stack in stacks]
    masks = (0,) + tuple(bits)
    ends, end_masks = [], []
    for held, order in zip(pieces, orders):
        late = other_pieces(held, wide, order)
        blocks = list(late.values())
        ends.append(blocks[0] if len(blocks) == 1 else jnp.stack(blocks))
        end_masks.append(tuple(late))

    for hop in range(1, hops):
        carried = choose(owners, along[hop - 1], carried, came, False, [dense, stacks[0]])
        came = [swap(block, wide, bit) for block, bit in zip(carried, along[hop])]
    carried = choose(owners, along[-1], carried, came, True, ends)
    other = swap(carried, wide, 1)
    ends = tie(ends, crossed_stacks)
    parts = []
    for which in range(2):
        parts.append((stacks[which], which, masks))
        parts.append((crossed_stacks[which], which, crossed(masks)))
        parts.append((ends[which], which, end_masks[which]))
        parts.append((swap(ends[which], wide, 1), which, crossed(end_masks[which])))

    total, count = block_sums(targets, tiles, received, features.shape[0])
    combined = combined_rows(dense, carried, other, total, count, features)
    return layer(combined, parts, second_weight.shape[0] * wide)


def solution(mesh):
    placed = (
        P(("wide", "narrow"), None),
        P(),
        P(("wide", "narrow"), None),
        P(("wide", "narrow"), None, None, None),
        P(("wide", "narrow"), None, None),
        P(("wide", "narrow"), None, None),
        P("wide", None),
        P("wide", None),
    )
    local = functools.partial(shards, wide=mesh.shape["wide"], narrow=mesh.shape["narrow"])
    return jax.shard_map(
        local, mesh=mesh, in_specs=placed, out_specs=P(("wide", "narrow"), None), check_vma=False
    )
```
